768 devices in a mesh: section: 24 (over y_hi, z), fsdp: 8 (over y_lo, core), tensor: 4 (over x).
Axes of the slice: x: 4, y: 8 (y_hi: 2, y_lo: 4; y = y_hi * 4 + y_lo), z: 12, core: 2. Of those that a mesh axis runs over, the one named last changes fastest.
Arguments:
- fresh: bfloat16 [2, 512, 2560], P(None, 'fsdp'), may hold values from -6 to 6
- sent: bfloat16 [24, 512, 2560], P('section', 'fsdp'), may hold values from -6 to 6
- stash: bfloat16 [24, 2, 512, 2560], P('section', None, 'fsdp'), may hold values from -6 to 6
- returned: bfloat16 [24, 512, 2560], P('section', 'fsdp'), may hold values from -6 to 6
- loss_grads: bfloat16 [2, 512, 2560], P(None, 'fsdp'), may hold values from -6 to 6
- plan: int32 [24, 2], P('section'), may hold values from 0 to 1
- frame_ids: int32 [2, 512], P(None, 'fsdp'), may hold values from 0 to 63, never falling along the last dimension, each value on 1 to 16 neighbouring positions
- qkv_weight: bfloat16 [24, 2560, 4096], P('section', 'fsdp', 'tensor'), may hold values from -0.125 to 0.125
- out_weight: bfloat16 [24, 2560, 2048], P('section', 'fsdp', 'tensor'), may hold values from -0.125 to 0.125
Outputs:
- activations_out: bfloat16 [24, 512, 2560], P('section', 'fsdp')
- cotangents_out: bfloat16 [24, 512, 2560], P('section', 'fsdp')
The draws below stay inside these ranges and needn't reach their ends.
Inputs may be any that keep to these rules, and one draw needn't show every extreme that they name: `frame_ids`: frame numbers never fall along the tokens; a frame holds 1 to 16 tokens, and some frame holds exactly 16.
All inputs are finite; a program needn't handle non-finite values.
Results may differ from the reference program's by a relative error of at most 0.02.
Values may be sent and summed in bfloat16 or wider, within the bound.
A program may use at most 64 MiB of HBM per device.

```python
import math
import jax
import jax.numpy as jnp
import numpy as np
from jax import lax

D = 2560
HQ = 16
KV = 8
HS = 128
MB_TOK = 64
TOKENS = 512
N_SECTION = 24
N_FSDP = 8
N_TENSOR = 4


def plant(drawn, rng, low, largest):
    index_at = [jax.random.randint(jax.random.fold_in(rng, axis), (), 0, length) for axis, length in enumerate(drawn.shape)]
    main_axis = drawn.shape.index(max(drawn.shape))
    next_to = index_at[:main_axis] + [(index_at[main_axis] + 1) % drawn.shape[main_axis]] + index_at[main_axis + 1:]
    return drawn.at[tuple(index_at)].set(low).at[tuple(next_to)].set(largest)


def block_levels(stream_key, dims, cuts, low, largest):
    loudness, own = 1.0, jax.random.fold_in(stream_key, 6)
    for dim, parts in cuts:
        heights = jnp.exp(jax.random.uniform(jax.random.fold_in(own, dim), (parts,), jnp.float32, low / len(cuts), largest / len(cuts)))
        loudness = loudness * jnp.repeat(heights, dims[dim] // parts).reshape([-1 if axis == dim else 1 for axis in range(len(dims))])
    return loudness


def split_up(number_of, total, limit, lean):
    loads = [(1 << 20) // math.isqrt(grade ** lean) + 1 for grade in range(2, number_of + 1)]
    rest, holding = total - limit - (number_of - 1), [1] * (number_of - 1)
    while rest > 0:
        movable = [i for i in range(number_of - 1) if holding[i] < limit]
        whole, budget = sum([loads[i] for i in movable]), rest
        for i in movable:
            addition = min(limit - holding[i], max(1, budget * loads[i] // whole), rest)
            holding[i] = holding[i] + addition
            rest = rest - addition
    return np.array([limit] + holding)


def uneven_parts(rng, amount, total, bound, lean):
    if amount == 2:
        one = jax.random.randint(rng, (), max(1, total - bound), min(bound, total - 1) + 1)
        return jnp.stack([one, total - one])
    lengths = jnp.asarray(split_up(amount, total, bound, lean), jnp.int32)
    twos = (amount - 1) // 2
    donor, sink = lengths[1:1 + 2 * twos:2], lengths[2:2 + 2 * twos:2]
    room = jnp.minimum(donor - 1, bound - sink)
    passed = jax.random.randint(jax.random.fold_in(rng, 1), (twos,), 0, 1 << 20) % (room + 1)
    lengths = lengths.at[1:1 + 2 * twos:2].set(donor - passed).at[2:2 + 2 * twos:2].set(sink + passed)
    return lengths[jax.random.permutation(jax.random.fold_in(rng, 2), amount)]


def gaussian(stream_key, dims, scale, limit, split=(), kind=jnp.bfloat16):
    array = jax.random.normal(stream_key, dims, jnp.float32) * scale
    if len(split) > 0:
        array = block_levels(stream_key, dims, split, -0.22, 0.18) * array
    return jnp.clip(array, min=-limit, max=limit).astype(kind)


def setup_inputs(seed: int = 0) -> dict:
    arg_keys = jax.random.split(jax.random.key(seed), 10)
    fresh = gaussian(arg_keys[0], (2, TOKENS, D), 1.0, 6.0, ((1, 8),))
    sent = gaussian(arg_keys[1], (N_SECTION, TOKENS, D), 1.0, 6.0, ((0, 24), (1, 8)))
    stash = gaussian(arg_keys[2], (N_SECTION, 2, TOKENS, D), 1.0, 6.0, ((0, 24), (2, 8)))
    returned = gaussian(arg_keys[3], (N_SECTION, TOKENS, D), 1.0, 6.0, ((0, 24), (1, 8)))
    loss_grads = gaussian(arg_keys[4], (2, TOKENS, D), 1.0, 6.0, ((1, 8),))
    plan = plant(jax.random.randint(arg_keys[5], (N_SECTION, 2), 0, 2), jax.random.fold_in(arg_keys[5], 1), 0, 1).astype(jnp.int32)
    frame_ids = jax.vmap(lambda own: jnp.searchsorted(jnp.cumsum(uneven_parts(own, TOKENS // 8, TOKENS, 16, 0)), jnp.arange(TOKENS), side="right"))(jax.random.split(arg_keys[6], 2)).reshape((2, TOKENS)).astype(jnp.int32)
    qkv_weight = gaussian(arg_keys[7], (N_SECTION, D, (HQ + 2 * KV) * HS), D ** -0.5, 0.125, ((0, 24), (1, 8), (2, 4)))
    out_weight = gaussian(arg_keys[8], (N_SECTION, D, HQ * HS), (HQ * HS) ** -0.5, 0.125, ((0, 24), (1, 8), (2, 4)))
    return dict(fresh=fresh, sent=sent, stash=stash, returned=returned, loss_grads=loss_grads, plan=plan, frame_ids=frame_ids, qkv_weight=qkv_weight, out_weight=out_weight)


def group_partial(x, wq, wo, frames):
    q_heads = wo.shape[1] // HS
    kv_heads = (wq.shape[1] // HS - q_heads) // 2
    rows = x.shape[0]
    xf = x.astype(jnp.float32)
    normed = (xf * lax.rsqrt(lax.optimization_barrier(jnp.mean(xf * xf, -1, keepdims=True)) + 1e-05)).astype(jnp.bfloat16)
    mixed = jnp.dot(normed, wq, preferred_element_type=jnp.float32).astype(jnp.bfloat16)
    mixed = mixed.reshape(rows, q_heads + 2 * kv_heads, HS)
    query = mixed[:, :q_heads].reshape(rows, kv_heads, q_heads // kv_heads, HS)
    keys = mixed[:, q_heads:q_heads + kv_heads]
    values = mixed[:, q_heads + kv_heads:]
    scores = jnp.einsum('tkgd,skd->kgts', query.astype(jnp.float32), keys.astype(jnp.float32)) * HS ** (-0.5)
    allowed = frames[None, :] <= frames[:, None]
    weights = jnp.where(allowed, jnp.exp(scores), 0.0)
    probs = (weights / lax.optimization_barrier(jnp.sum(weights, -1, keepdims=True))).astype(jnp.bfloat16)
    context = jnp.einsum('kgts,skd->tkgd', probs.astype(jnp.float32), values.astype(jnp.float32))
    context = context.astype(jnp.bfloat16).reshape(rows, q_heads * HS)
    return lax.dot_general(context, wo, (((1,), (1,)), ((), ())), preferred_element_type=jnp.float32)

def back_group(x, grad, wq, wo, frames):
    _, pull = jax.vjp(lambda a: group_partial(a, wq, wo, frames), x)
    return pull(grad.astype(jnp.float32))[0]

def split_weights(wq_all, wo_all):
    wq_parts = wq_all.reshape(D, N_TENSOR, -1).transpose(1, 0, 2)
    wo_parts = wo_all.reshape(D, N_TENSOR, -1).transpose(1, 0, 2)
    return (wq_parts, wo_parts)

def apply_layer(x, wq_all, wo_all, frames):
    groups = x.reshape(N_FSDP, MB_TOK, D)
    marks = frames.reshape(N_FSDP, MB_TOK)
    wq_parts, wo_parts = split_weights(wq_all, wo_all)
    per_tensor = jax.vmap(group_partial, in_axes=(None, 0, 0, None))
    terms = jax.vmap(per_tensor, in_axes=(0, None, None, 0))(groups, wq_parts, wo_parts, marks)
    rounded = lax.optimization_barrier(terms.astype(jnp.bfloat16))
    total = lax.optimization_barrier(jnp.sum(rounded.astype(jnp.float32), axis=1))
    return (groups.astype(jnp.float32) + total).astype(jnp.bfloat16).reshape(TOKENS, D)

def back_layer(x, grad, wq_all, wo_all, frames):
    groups = x.reshape(N_FSDP, MB_TOK, D)
    grads = grad.reshape(N_FSDP, MB_TOK, D)
    marks = frames.reshape(N_FSDP, MB_TOK)
    wq_parts, wo_parts = split_weights(wq_all, wo_all)
    per_tensor = jax.vmap(back_group, in_axes=(None, None, 0, 0, None))
    dx_p = jax.vmap(per_tensor, in_axes=(0, 0, None, None, 0))(groups, grads, wq_parts, wo_parts, marks)
    total = lax.optimization_barrier(jnp.sum(dx_p.astype(jnp.float32), axis=1))
    return (grads.astype(jnp.float32) + total).astype(jnp.bfloat16).reshape(TOKENS, D)

def reference(fresh, sent, stash, returned, loss_grads, plan, frame_ids, qkv_weight, out_weight):

    def forward_all(inputs, frames):
        return lax.map(lambda a: apply_layer(a[0], a[1], a[2], frames), (inputs, qkv_weight, out_weight))
    section_ids = jnp.arange(N_SECTION, dtype=jnp.int32)

    def backward_all(cot, slots):
        saved = stash[section_ids, slots]
        marks = frame_ids[slots]
        return lax.map(lambda a: back_layer(a[0], a[1], a[2], a[3], a[4]), (saved, cot, qkv_weight, out_weight, marks))
    first_out = forward_all(jnp.concatenate([fresh[:1], sent[:-1]], axis=0), frame_ids[0])
    activations_out = forward_all(jnp.concatenate([fresh[1:2], first_out[:-1]], axis=0), frame_ids[1])
    dx_one = backward_all(jnp.concatenate([returned[1:], loss_grads[:1]], axis=0), plan[:, 0])
    dx_two = backward_all(jnp.concatenate([dx_one[1:], loss_grads[1:2]], axis=0), plan[:, 1])
    return (activations_out, dx_two)
```

```python
import jax
import jax.numpy as jnp
from jax import lax
from jax.experimental import pallas as pl
from jax.experimental.pallas import tpu as pltpu
from jax.sharding import PartitionSpec as P

HS = 128
MESH = pl.DeviceIdType.MESH
BF = jnp.bfloat16
F32 = jnp.float32
PARTS = 2
WIDE = 512


def nn(a, b):
    return jnp.dot(a, b, preferred_element_type=F32)


def nt(a, b):
    return lax.dot_general(a, b, (((1,), (1,)), ((), ())), preferred_element_type=F32)


def tn(a, b):
    return lax.dot_general(a, b, (((0,), (0,)), ((), ())), preferred_element_type=F32)


def kernel(
    fresh, sent, stash, returned, loss, plan, frames, wq, wo, out_f, out_b,
    WQ, WO, X1, X2, ST, SB, G1, G2, XN, RN, MX, PR, CT, DC, DM, PP, RB, HOP, SL, own_sem, line_send, line_recv,
    sib_send, sib_recv, loc_sem, hop_send, hop_recv, ag_send, ag_recv, rs_send, rs_recv,
):
    s = lax.axis_index("section")
    f = lax.axis_index("fsdp")
    t = lax.axis_index("tensor")
    ns, nt_ = lax.axis_size("section"), lax.axis_size("tensor")
    ny = lax.axis_size("fsdp") // 2
    y, core = f // 2, lax.rem(f, 2)
    sibling = 2 * y + 1 - core
    rows, width = X1.shape
    cut = rows // nt_
    depth = wq.shape[1]
    piece = depth // PARTS
    qh = WO.shape[1] // HS
    kh = (WQ.shape[1] // HS - qh) // 2
    group = qh // kh
    scale = HS**-0.5
    first, last = s == 0, s == ns - 1
    mine = pl.ds(pl.multiple_of(t * cut, cut), cut)

    def remote(src, dst, ss, rs, **where):
        return pltpu.make_async_remote_copy(
            src_ref=src, dst_ref=dst, send_sem=ss, recv_sem=rs, device_id=where, device_id_type=MESH
        )

    barrier = pltpu.get_barrier_semaphore()

    def greet(**where):
        pl.semaphore_signal(barrier, inc=1, device_id=where, device_id_type=MESH)

    greet(fsdp=sibling)
    for k in range(1, nt_):
        greet(tensor=lax.rem(t + k, nt_))
    pl.when(y > 0)(lambda: greet(fsdp=f - 2))
    pl.when(y < ny - 1)(lambda: greet(fsdp=f + 2))
    pl.when(s > 0)(lambda: greet(section=s - 1))
    pl.when(s < ns - 1)(lambda: greet(section=s + 1))
    partners = nt_ + jnp.where(y > 0, 1, 0) + jnp.where(y < ny - 1, 1, 0)
    partners = partners + jnp.where(s > 0, 1, 0) + jnp.where(s < ns - 1, 1, 0)
    pl.semaphore_wait(barrier, partners)

    def home(block, n):
        here, there = (wq, WQ) if n < PARTS else (wo, WO)
        at = (n % PARTS) * piece
        row = pl.multiple_of((2 * block + core) * depth + at, 16)
        return here.at[0, pl.ds(at, piece)], there.at[pl.ds(row, piece)]

    def far(block, n):
        there = WQ if n < PARTS else WO
        row = pl.multiple_of((2 * block + 1 - core) * depth + (n % PARTS) * piece, 16)
        return there.at[pl.ds(row, piece)]

    def own_sends(n):
        here, there = home(y, n)
        up = remote(here, there, own_sem.at[0, n], line_recv.at[0, 0, n], fsdp=jnp.minimum(f + 2, 2 * ny - 1))
        down = remote(here, there, own_sem.at[1, n], line_recv.at[1, 0, n], fsdp=jnp.maximum(f - 2, 0))
        over = remote(here, there, own_sem.at[2, n], sib_recv.at[0, ny - 1, n], fsdp=sibling)
        return up, down, over

    def start_own(n):
        up, down, over = own_sends(n)
        pl.when(y < ny - 1)(lambda: up.start())
        pl.when(y > 0)(lambda: down.start())
        over.start()

    def finish_own(n):
        up, down, over = own_sends(n)
        pl.when(y < ny - 1)(lambda: up.wait_send())
        pl.when(y > 0)(lambda: down.wait_send())
        over.wait_send()

    def line(d, j, n):
        block = y - 1 - j if d == 0 else y + 1 + j
        valid = block >= 0 if d == 0 else block <= ny - 1
        goes_on = jnp.logical_and(valid, y < ny - 1 if d == 0 else y > 0)
        block = jnp.clip(block, 0, ny - 1)
        there = home(block, n)[1]
        onward = jnp.clip(f + (2 if d == 0 else -2), 0, 2 * ny - 1)
        nxt = None
        if j < ny - 2:
            nxt = remote(there, there, line_send.at[d, j, n], line_recv.at[d, j + 1, n], fsdp=onward)
        got = remote(there, there, line_send.at[d, j, n], line_recv.at[d, j, n], fsdp=sibling)
        over = remote(there, there, sib_send.at[d, j, n], sib_recv.at[d, j, n], fsdp=sibling)
        other = far(block, n)
        sib = remote(other, other, sib_send.at[d, j, n], sib_recv.at[d, j, n], fsdp=sibling)
        return valid, goes_on, got, nxt, over, sib

    def relay(j, n):
        for d in range(2):
            valid, goes_on, got, nxt, over, _ = line(d, j, n)

            @pl.when(valid)
            def _():
                got.wait_recv()

            if nxt is not None:
                pl.when(goes_on)(lambda: nxt.start())
            pl.when(valid)(lambda: over.start())

    def finish_line(j, n):
        for d in range(2):
            valid, goes_on, _, nxt, over, _ = line(d, j, n)
            if nxt is not None:
                pl.when(goes_on)(lambda: nxt.wait_send())
            pl.when(valid)(lambda: over.wait_send())

    def from_sibling(n):
        other = far(y, n)
        remote(other, other, own_sem.at[2, n], sib_recv.at[0, ny - 1, n], fsdp=sibling).wait_recv()
        for j in range(ny - 1):
            for d in range(2):
                valid, _, _, _, _, sib = line(d, j, n)
                pl.when(valid)(lambda: sib.wait_recv())

    for n in range(PARTS):
        start_own(n)

    own_q = pltpu.make_async_copy(wq.at[0], WQ.at[pl.ds(pl.multiple_of(f * depth, 16), depth)], loc_sem.at[0])
    own_o = pltpu.make_async_copy(wo.at[0], WO.at[pl.ds(pl.multiple_of(f * depth, 16), depth)], loc_sem.at[1])
    saved = pltpu.make_async_copy(stash.at[0], ST, loc_sem.at[2])
    saved.start()
    own_q.start()
    own_o.start()

    def hop_down(i, src):
        return remote(src, HOP.at[i], hop_send.at[i], hop_recv.at[i], section=jnp.minimum(s + 1, ns - 1))

    def hop_up(i, src):
        return remote(src, HOP.at[i], hop_send.at[i], hop_recv.at[i], section=jnp.maximum(s - 1, 0))

    sent_hop = hop_down(0, sent.at[0, mine])
    ret_hop = hop_up(2, returned.at[0, mine])
    pl.when(s < ns - 1)(lambda: sent_hop.start())
    pl.when(s > 0)(lambda: ret_hop.start())
    fresh_in = [
        pltpu.make_async_copy(fresh.at[0], X1, loc_sem.at[3]), pltpu.make_async_copy(fresh.at[1], X2, loc_sem.at[4])
    ]
    loss_in = [
        pltpu.make_async_copy(loss.at[0], G1, loc_sem.at[5]), pltpu.make_async_copy(loss.at[1], G2, loc_sem.at[6])
    ]

    @pl.when(first)
    def _():
        for c in fresh_in:
            c.start()

    @pl.when(last)
    def _():
        for c in loss_in:
            c.start()

    far_first = sorted(range(1, nt_), key=lambda k: -min(k, nt_ - k))

    def spread(i, src, dst_at):
        return [
            remote(src, dst_at, ag_send.at[i, k - 1], ag_recv.at[i, k - 1], tensor=lax.rem(t + k, nt_)) for k in far_first
        ]

    def spread_in(i, dst):
        return [
            remote(at, at, ag_send.at[i, k - 1], ag_recv.at[i, k - 1], tensor=lax.rem(t + k, nt_))
            for k in far_first
            for at in (dst.at[pl.ds(pl.multiple_of(lax.rem(t + nt_ - k, nt_) * cut, cut), cut)],)
        ]

    def gather_start(i, got, dst):
        got.wait_recv()
        for c in spread(i, HOP.at[i], dst.at[mine]):
            c.start()
        dst[mine, :] = HOP[i]

    def gather_finish(i, dst):
        for c in spread_in(i, dst):
            c.wait_recv()
        for c in spread(i, HOP.at[i], dst.at[mine]):
            c.wait_send()

    def norm(x):
        xf = x.astype(F32)
        r = lax.rsqrt(jnp.mean(xf * xf, -1, keepdims=True) + 1e-05)
        return (xf * r).astype(BF), r

    def allowed(fr):
        fr = jnp.broadcast_to(fr, (rows, rows))
        ok = jnp.where(fr <= fr.T, 1.0, 0.0)
        return jnp.concatenate([ok] * group, axis=0) > 0.5

    def chosen(tick, a, b):
        w = plan[0, tick].astype(F32)
        return a.astype(F32) * (1.0 - w) + b.astype(F32) * w

    fr_in = frames[...].astype(F32)

    def project(m0, m1, x):
        def block(i, carry):
            cols = pl.ds(pl.multiple_of(i * WIDE, 128), WIDE)
            MX[m0:m1, cols] = nn(x[...], WQ[:, cols]).astype(BF)
            return carry

        lax.fori_loop(0, WQ.shape[1] // WIDE, block, 0)

    def heads(ref, m0, first_head):
        return jnp.concatenate(
            [ref[m0 : m0 + rows, (first_head + g) * HS : (first_head + g + 1) * HS] for g in range(group)], axis=0
        )

    def probs(m0, k, ok):
        q = heads(MX, m0, k * group)
        key = MX[m0 : m0 + rows, (qh + k) * HS : (qh + k + 1) * HS]
        w = jnp.where(ok, jnp.exp(nt(q, key) * scale), 0.0)
        return w / jnp.sum(w, -1, keepdims=True)

    def attend(m0, ok):
        for k in range(kh):
            p = probs(m0, k, ok).astype(BF)
            ctx = nn(p, MX[m0 : m0 + rows, (qh + kh + k) * HS : (qh + kh + k + 1) * HS]).astype(BF)
            for g in range(group):
                CT[:, (k * group + g) * HS : (k * group + g + 1) * HS] = ctx[g * rows : (g + 1) * rows]

    def send_out(i):
        return [
            remote(
                PP.at[i, pl.ds(pl.multiple_of(lax.rem(t + k, nt_) * cut, cut), cut)], RB.at[i, k - 1],
                rs_send.at[i, k - 1], rs_recv.at[i, k - 1], tensor=lax.rem(t + k, nt_),
            )
            for k in far_first
        ]

    def output(i):
        def block(j, carry):
            cols = pl.ds(pl.multiple_of(j * WIDE, 128), WIDE)
            PP[i, :, cols] = nt(CT[...], WO[cols, :]).astype(BF)
            return carry

        lax.fori_loop(0, width // WIDE, block, 0)
        for c in send_out(i):
            c.start()

    def reduced(i, base):
        for c in send_out(i):
            c.wait_recv()
        total = PP[i, mine, :].astype(F32)
        for k in range(1, nt_):
            total = total + RB[i, k - 1].astype(F32)
        SL[i] = (base[mine, :].astype(F32) + total).astype(BF)

    def backward(i, tick, grad):
        m0 = (1 + tick) * rows
        DC[...] = nn(grad[...], WO[...]).astype(BF)
        dots = jnp.zeros((rows, 1), F32)
        for k in range(kh):
            value = MX[m0 : m0 + rows, (qh + kh + k) * HS : (qh + kh + k + 1) * HS]
            key = MX[m0 : m0 + rows, (qh + k) * HS : (qh + k + 1) * HS]
            q = heads(MX, m0, k * group)
            dctx = heads(DC, 0, k * group)
            p = PR[tick, k]
            dp = nt(dctx, value).astype(BF).astype(F32)
            ds = (p * (dp - jnp.sum(dp * p, -1, keepdims=True)) * scale).astype(BF)
            dq = nn(ds, key).astype(BF)
            dk = tn(ds, q).astype(BF)
            dv = tn(p.astype(BF), dctx).astype(BF)
            for g in range(group):
                DM[:, (k * group + g) * HS : (k * group + g + 1) * HS] = dq[g * rows : (g + 1) * rows]
            DM[:, (qh + k) * HS : (qh + k + 1) * HS] = dk
            DM[:, (qh + kh + k) * HS : (qh + kh + k + 1) * HS] = dv
        mean = jnp.sum(DM[...].astype(F32) * MX[m0 : m0 + rows, :].astype(F32), -1, keepdims=True) / width
        r = RN[tick][:, 0:1]

        def block(j, carry):
            cols = pl.ds(pl.multiple_of(j * WIDE, 128), WIDE)
            dn = nt(DM[...], WQ[cols, :]).astype(BF).astype(F32)
            xn = SB[tick, :, cols].astype(F32) * r
            PP[i, :, cols] = (r * (dn - xn * mean)).astype(BF)
            return carry

        lax.fori_loop(0, width // WIDE, block, 0)
        for c in send_out(i):
            c.start()

    saved.wait()
    for tick in range(2):
        x = chosen(tick, ST[0], ST[1]).astype(BF)
        SB[tick] = x
        xn, r = norm(x)
        XN[(1 + tick) * rows : (2 + tick) * rows, :] = xn
        RN[tick] = jnp.broadcast_to(r, (rows, HS))
    for n in range(PARTS):
        relay(0, n)
    for n in range(PARTS, 2 * PARTS):
        start_own(n)
    pl.when(s > 0)(lambda: gather_start(0, sent_hop, X1))
    pl.when(s < ns - 1)(lambda: gather_start(2, ret_hop, G1))
    for j in range(1, ny - 1):
        for n in range(PARTS):
            relay(j, n)
    pl.when(s > 0)(lambda: gather_finish(0, X1))
    pl.when(s < ns - 1)(lambda: gather_finish(2, G1))

    @pl.when(first)
    def _():
        for c in fresh_in:
            c.wait()

    @pl.when(last)
    def _():
        for c in loss_in:
            c.wait()

    XN[0:rows, :] = norm(X1[...])[0]
    between = jnp.logical_and(y > 0, y < ny - 1)

    def relay_out():
        for j in range(ny - 1):
            for n in range(PARTS, 2 * PARTS):
                relay(j, n)

    pl.when(between)(relay_out)
    own_q.wait()
    for n in range(PARTS):
        from_sibling(n)
    project(0, 3 * rows, XN)
    attend(0, allowed(fr_in[0:1]))
    for tick in range(2):
        ok = allowed(chosen(tick, fr_in[0:1], fr_in[1:2]))
        for k in range(kh):
            PR[tick, k] = probs((1 + tick) * rows, k, ok)
    pl.when(jnp.logical_not(between))(relay_out)
    own_o.wait()
    for n in range(PARTS, 2 * PARTS):
        from_sibling(n)

    output(0)
    backward(2, 0, G1)
    reduced(0, X1)
    down = hop_down(1, SL.at[0])
    pl.when(s < ns - 1)(lambda: down.start())
    reduced(2, G1)
    up = hop_up(3, SL.at[2])
    pl.when(s > 0)(lambda: up.start())

    pl.when(s > 0)(lambda: gather_start(1, down, X2))
    pl.when(s < ns - 1)(lambda: gather_start(3, up, G2))
    pl.when(s > 0)(lambda: gather_finish(1, X2))
    XN[0:rows, :] = norm(X2[...])[0]
    project(0, rows, XN.at[0:rows])
    attend(0, allowed(fr_in[1:2]))
    output(1)
    pl.when(s < ns - 1)(lambda: gather_finish(3, G2))
    backward(3, 1, G2)
    results = []
    for i, base, out, sem in ((1, X2, out_f, 7), (3, G2, out_b, 8)):
        reduced(i, base)
        keep = pltpu.make_async_copy(SL.at[i], out.at[0, mine], loc_sem.at[sem])
        copies = spread(3 + i // 2 + 1, SL.at[i], out.at[0, mine])
        for c in copies:
            c.start()
        keep.start()
        results.append((keep, copies, spread_in(3 + i // 2 + 1, out.at[0])))
    for keep, copies, arriving in results:
        for c in arriving:
            c.wait_recv()
        for c in copies:
            c.wait_send()
        keep.wait()

    for i in range(4):
        for c in send_out(i):
            c.wait_send()
    for c in (sent_hop, down):
        pl.when(s < ns - 1)(lambda: c.wait_send())
    for c in (ret_hop, up):
        pl.when(s > 0)(lambda: c.wait_send())
    for n in range(2 * PARTS):
        finish_own(n)
        for j in range(ny - 1):
            finish_line(j, n)


def body(fresh, sent, stash, returned, loss_grads, plan, frame_ids, qkv_weight, out_weight):
    nt_ = lax.axis_size("tensor")
    n_fsdp = lax.axis_size("fsdp")
    ny = n_fsdp // 2
    _, rows, width = sent.shape
    depth, columns = qkv_weight.shape[1:]
    inner = out_weight.shape[2]
    kh = (columns - inner) // (2 * HS)
    group = inner // HS // kh
    cut = rows // nt_
    dma = pltpu.SemaphoreType.DMA
    anywhere = pl.BlockSpec(memory_space=pl.ANY)
    whole = pl.BlockSpec(memory_space=pltpu.VMEM)
    act = pltpu.VMEM((rows, width), BF)
    acts = pltpu.VMEM((2, rows, width), BF)
    return pl.pallas_call(
        kernel,
        out_shape=[jax.ShapeDtypeStruct(sent.shape, BF)] * 2,
        in_specs=[anywhere] * 5 + [pl.BlockSpec(memory_space=pltpu.SMEM), whole] + [anywhere] * 2,
        out_specs=[anywhere] * 2,
        scratch_shapes=[
            pltpu.VMEM((n_fsdp * depth, columns), BF),
            pltpu.VMEM((n_fsdp * depth, inner), BF),
            act, act, acts, acts, act, act,
            pltpu.VMEM((3 * rows, width), BF),
            pltpu.VMEM((2, rows, HS), F32),
            pltpu.VMEM((3 * rows, columns), BF),
            pltpu.VMEM((2, kh, group * rows, rows), F32),
            pltpu.VMEM((rows, inner), BF),
            pltpu.VMEM((rows, inner), BF),
            pltpu.VMEM((rows, columns), BF),
            pltpu.VMEM((4, rows, width), BF),
            pltpu.VMEM((4, nt_ - 1, cut, width), BF),
            pltpu.VMEM((4, cut, width), BF),
            pltpu.VMEM((4, cut, width), BF),
            dma((3, 2 * PARTS)),
            dma((2, ny - 1, 2 * PARTS)),
            dma((2, ny - 1, 2 * PARTS)),
            dma((2, ny - 1, 2 * PARTS)),
            dma((2, ny, 2 * PARTS)),
            dma((9,)),
            dma((4,)),
            dma((4,)),
            dma((6, nt_ - 1)),
            dma((6, nt_ - 1)),
            dma((4, nt_ - 1)),
            dma((4, nt_ - 1)),
        ],
        compiler_params=pltpu.CompilerParams(
            collective_id=0, has_side_effects=True, vmem_limit_bytes=40 << 20
        ),
        name="relay",
    )(fresh, sent, stash, returned, loss_grads, plan, frame_ids, qkv_weight, out_weight)


def solution(mesh):
    placed = (
        P(None, "fsdp", None),
        P("section", "fsdp", None),
        P("section", None, "fsdp", None),
        P("section", "fsdp", None),
        P(None, "fsdp", None),
        P("section", None),
        P(None, "fsdp"),
        P("section", "fsdp", "tensor"),
        P("section", "fsdp", "tensor"),
    )
    return jax.shard_map(
        body,
        mesh=mesh,
        in_specs=placed,
        out_specs=(P("section", "fsdp", None), P("section", "fsdp", None)),
        check_vma=False,
    )
```

```python
import jax
import jax.numpy as jnp
from jax import lax
from jax.experimental import pallas as pl
from jax.experimental.pallas import tpu as pltpu
from jax.sharding import PartitionSpec as P

HS = 128
MESH = pl.DeviceIdType.MESH
BF = jnp.bfloat16
F32 = jnp.float32
PARTS = 2
WIDE = 512


def nn(a, b):
    return jnp.dot(a, b, preferred_element_type=F32)


def nt(a, b):
    return lax.dot_general(a, b, (((1,), (1,)), ((), ())), preferred_element_type=F32)


def tn(a, b):
    return lax.dot_general(a, b, (((0,), (0,)), ((), ())), preferred_element_type=F32)


def kernel(
    fresh, sent, stash, returned, loss, plan, frames, wq, wo, out_f, out_b,
    WQ, WO, WT, X1, X2, ST, SB, G1, G2, XN, RN, MX, PR, CT, DM, DA, PP, RB, HOP, SL, own_sem, line_send, line_recv,
    sib_send, sib_recv, loc_sem, hop_send, hop_recv, ag_send, ag_recv, rs_send, rs_recv,
):
    s = lax.axis_index("section")
    f = lax.axis_index("fsdp")
    t = lax.axis_index("tensor")
    ns, nt_ = lax.axis_size("section"), lax.axis_size("tensor")
    ny = lax.axis_size("fsdp") // 2
    y, core = f // 2, lax.rem(f, 2)
    sibling = 2 * y + 1 - core
    rows, width = X1.shape
    cut = rows // nt_
    depth = wq.shape[1]
    piece = depth // PARTS
    qh = WO.shape[1] // HS
    kh = (WQ.shape[1] // HS - qh) // 2
    group = qh // kh
    scale = HS**-0.5
    first, last = s == 0, s == ns - 1
    mine = pl.ds(pl.multiple_of(t * cut, cut), cut)
    wide = width // ny

    def cols(b):
        return pl.ds(pl.multiple_of(b * wide, 128), wide)

    def remote(src, dst, ss, rs, **where):
        return pltpu.make_async_remote_copy(
            src_ref=src, dst_ref=dst, send_sem=ss, recv_sem=rs, device_id=where, device_id_type=MESH
        )

    barrier = pltpu.get_barrier_semaphore()

    def greet(**where):
        pl.semaphore_signal(barrier, inc=1, device_id=where, device_id_type=MESH)

    greet(fsdp=sibling)
    for k in range(1, nt_):
        greet(tensor=lax.rem(t + k, nt_))
    pl.when(y > 0)(lambda: greet(fsdp=f - 2))
    pl.when(y < ny - 1)(lambda: greet(fsdp=f + 2))
    pl.when(s > 0)(lambda: greet(section=s - 1))
    pl.when(s < ns - 1)(lambda: greet(section=s + 1))
    partners = nt_ + jnp.where(y > 0, 1, 0) + jnp.where(y < ny - 1, 1, 0)
    partners = partners + jnp.where(s > 0, 1, 0) + jnp.where(s < ns - 1, 1, 0)
    pl.semaphore_wait(barrier, partners)

    def home(block, n):
        here, there = (wq, WQ) if n < PARTS else (wo, WO)
        at = (n % PARTS) * piece
        row = pl.multiple_of((2 * block + core) * depth + at, 16)
        return here.at[0, pl.ds(at, piece)], there.at[pl.ds(row, piece)]

    def far(block, n):
        there = WQ if n < PARTS else WO
        row = pl.multiple_of((2 * block + 1 - core) * depth + (n % PARTS) * piece, 16)
        return there.at[pl.ds(row, piece)]

    def own_sends(n):
        here, there = home(y, n)
        up = remote(here, there, own_sem.at[0, n], line_recv.at[0, 0, n], fsdp=jnp.minimum(f + 2, 2 * ny - 1))
        down = remote(here, there, own_sem.at[1, n], line_recv.at[1, 0, n], fsdp=jnp.maximum(f - 2, 0))
        over = remote(here, there, own_sem.at[2, n], sib_recv.at[0, ny - 1, n], fsdp=sibling)
        return up, down, over

    def start_own(n):
        up, down, over = own_sends(n)
        pl.when(y < ny - 1)(lambda: up.start())
        pl.when(y > 0)(lambda: down.start())
        over.start()

    def finish_own(n):
        up, down, over = own_sends(n)
        pl.when(y < ny - 1)(lambda: up.wait_send())
        pl.when(y > 0)(lambda: down.wait_send())
        over.wait_send()

    def line(d, j, n):
        block = y - 1 - j if d == 0 else y + 1 + j
        valid = block >= 0 if d == 0 else block <= ny - 1
        goes_on = jnp.logical_and(valid, y < ny - 1 if d == 0 else y > 0)
        block = jnp.clip(block, 0, ny - 1)
        there = home(block, n)[1]
        onward = jnp.clip(f + (2 if d == 0 else -2), 0, 2 * ny - 1)
        nxt = None
        if j < ny - 2:
            nxt = remote(there, there, line_send.at[d, j, n], line_recv.at[d, j + 1, n], fsdp=onward)
        got = remote(there, there, line_send.at[d, j, n], line_recv.at[d, j, n], fsdp=sibling)
        over = remote(there, there, sib_send.at[d, j, n], sib_recv.at[d, j, n], fsdp=sibling)
        other = far(block, n)
        sib = remote(other, other, sib_send.at[d, j, n], sib_recv.at[d, j, n], fsdp=sibling)
        return valid, goes_on, got, nxt, over, sib

    def relay(j, n):
        for d in range(2):
            valid, goes_on, got, nxt, over, _ = line(d, j, n)

            @pl.when(valid)
            def _():
                got.wait_recv()

            if nxt is not None:
                pl.when(goes_on)(lambda: nxt.start())
            pl.when(valid)(lambda: over.start())

    def finish_line(j, n):
        for d in range(2):
            valid, goes_on, _, nxt, over, _ = line(d, j, n)
            if nxt is not None:
                pl.when(goes_on)(lambda: nxt.wait_send())
            pl.when(valid)(lambda: over.wait_send())

    def own_from_sibling(n):
        other = far(y, n)
        remote(other, other, own_sem.at[2, n], sib_recv.at[0, ny - 1, n], fsdp=sibling).wait_recv()

    def from_sibling(j, n):
        for d in range(2):
            valid, _, _, _, _, sib = line(d, j, n)
            pl.when(valid)(lambda: sib.wait_recv())

    for n in range(PARTS):
        start_own(n)

    own_q = pltpu.make_async_copy(wq.at[0], WQ.at[pl.ds(pl.multiple_of(f * depth, 16), depth)], loc_sem.at[0])
    own_o = pltpu.make_async_copy(wo.at[0], WO.at[pl.ds(pl.multiple_of(f * depth, 16), depth)], loc_sem.at[1])
    saved = pltpu.make_async_copy(stash.at[0], ST, loc_sem.at[2])
    saved.start()
    own_q.start()
    own_o.start()

    everything = pl.ds(0, width)

    def hop_down(i, src, b=0):
        at = everything if i == 0 else cols(b)
        return remote(src.at[:, at], HOP.at[i, :, at], hop_send.at[i, b], hop_recv.at[i, b], section=jnp.minimum(s + 1, ns - 1))

    def hop_up(i, src, b=0):
        at = everything if i == 2 else cols(b)
        return remote(src.at[:, at], HOP.at[i, :, at], hop_send.at[i, b], hop_recv.at[i, b], section=jnp.maximum(s - 1, 0))

    sent_hop = hop_down(0, sent.at[0, mine])
    ret_hop = hop_up(2, returned.at[0, mine])
    pl.when(s < ns - 1)(lambda: sent_hop.start())
    pl.when(s > 0)(lambda: ret_hop.start())
    fresh_in = [
        pltpu.make_async_copy(fresh.at[0], X1, loc_sem.at[3]), pltpu.make_async_copy(fresh.at[1], X2, loc_sem.at[4])
    ]
    loss_in = [
        pltpu.make_async_copy(loss.at[0], G1, loc_sem.at[5]), pltpu.make_async_copy(loss.at[1], G2, loc_sem.at[6])
    ]

    @pl.when(first)
    def _():
        for c in fresh_in:
            c.start()

    @pl.when(last)
    def _():
        for c in loss_in:
            c.start()

    far_first = sorted(range(1, nt_), key=lambda k: -min(k, nt_ - k))

    def spread(i, src, dst, at, b=0):
        return [
            remote(
                src.at[:, at], dst.at[mine, at], ag_send.at[i, k - 1, b], ag_recv.at[i, k - 1, b], tensor=lax.rem(t + k, nt_)
            )
            for k in far_first
        ]

    def spread_in(i, dst, at, b=0):
        copies = []
        for k in far_first:
            there = dst.at[pl.ds(pl.multiple_of(lax.rem(t + nt_ - k, nt_) * cut, cut), cut), at]
            copies.append(
                remote(there, there, ag_send.at[i, k - 1, b], ag_recv.at[i, k - 1, b], tensor=lax.rem(t + k, nt_))
            )
        return copies

    def gather_start(i, got, dst, at, b=0):
        got.wait_recv()
        for c in spread(i, HOP.at[i], dst, at, b):
            c.start()
        dst[mine, at] = HOP[i, :, at]

    def gather_finish(i, dst, at, b=0):
        for c in spread_in(i, dst, at, b):
            c.wait_recv()

    def gather_sent(i, dst, at, b=0):
        for c in spread(i, HOP.at[i], dst, at, b):
            c.wait_send()

    def norm(x):
        xf = x.astype(F32)
        r = lax.rsqrt(jnp.mean(xf * xf, -1, keepdims=True) + 1e-05)
        return (xf * r).astype(BF), r

    def allowed(fr):
        fr = jnp.broadcast_to(fr, (rows, rows))
        ok = jnp.where(fr <= fr.T, 1.0, 0.0)
        return jnp.concatenate([ok] * group, axis=0) > 0.5

    def chosen(tick, a, b):
        w = plan[0, tick].astype(F32)
        return a.astype(F32) * (1.0 - w) + b.astype(F32) * w

    fr_in = frames[...].astype(F32)

    def project(m0, m1, x):
        def block(i, carry):
            cols = pl.ds(pl.multiple_of(i * WIDE, 128), WIDE)
            MX[m0:m1, cols] = nn(x[...], WQ[:, cols]).astype(BF)
            return carry

        lax.fori_loop(0, WQ.shape[1] // WIDE, block, 0)

    def heads(ref, m0, first_head):
        return jnp.concatenate(
            [ref[m0 : m0 + rows, (first_head + g) * HS : (first_head + g + 1) * HS] for g in range(group)], axis=0
        )

    def probs(m0, k, ok):
        q = heads(MX, m0, k * group)
        key = MX[m0 : m0 + rows, (qh + k) * HS : (qh + k + 1) * HS]
        w = jnp.where(ok, jnp.exp(nt(q, key) * scale), 0.0)
        return w / jnp.sum(w, -1, keepdims=True)

    def attend(m0, ok):
        for k in range(kh):
            p = probs(m0, k, ok).astype(BF)
            ctx = nn(p, MX[m0 : m0 + rows, (qh + kh + k) * HS : (qh + kh + k + 1) * HS]).astype(BF)
            for g in range(group):
                CT[:, (k * group + g) * HS : (k * group + g + 1) * HS] = ctx[g * rows : (g + 1) * rows]

    def send_out(i, b):
        return [
            remote(
                PP.at[i, pl.ds(pl.multiple_of(lax.rem(t + k, nt_) * cut, cut), cut), cols(b)],
                RB.at[i, k - 1, :, cols(b)],
                rs_send.at[i, k - 1, b], rs_recv.at[i, k - 1, b], tensor=lax.rem(t + k, nt_),
            )
            for k in far_first
        ]

    def output(i, b):
        PP[i, :, cols(b)] = nt(CT[...], WO[cols(b), :]).astype(BF)
        for c in send_out(i, b):
            c.start()

    def reduced(i, base, b):
        for c in send_out(i, b):
            c.wait_recv()
        total = PP[i, mine, cols(b)].astype(F32)
        for k in range(1, nt_):
            total = total + RB[i, k - 1, :, cols(b)].astype(F32)
        SL[i, :, cols(b)] = (base[mine, cols(b)].astype(F32) + total).astype(BF)

    def heads_back(tick, dc):
        m0 = (1 + tick) * rows
        for k in range(kh):
            value = MX[m0 : m0 + rows, (qh + kh + k) * HS : (qh + kh + k + 1) * HS]
            key = MX[m0 : m0 + rows, (qh + k) * HS : (qh + k + 1) * HS]
            q = heads(MX, m0, k * group)
            dctx = jnp.concatenate(
                [dc[:, (k * group + g) * HS : (k * group + g + 1) * HS] for g in range(group)], axis=0
            )
            p = PR[tick, k]
            dp = nt(dctx, value).astype(BF).astype(F32)
            ds = (p * (dp - jnp.sum(dp * p, -1, keepdims=True)) * scale).astype(BF)
            dq = nn(ds, key).astype(BF)
            dk = tn(ds, q).astype(BF)
            dv = tn(p.astype(BF), dctx).astype(BF)
            for g in range(group):
                DM[:, (k * group + g) * HS : (k * group + g + 1) * HS] = dq[g * rows : (g + 1) * rows]
            DM[:, (qh + k) * HS : (qh + k + 1) * HS] = dk
            DM[:, (qh + kh + k) * HS : (qh + kh + k + 1) * HS] = dv
        return jnp.sum(DM[...].astype(F32) * MX[m0 : m0 + rows, :].astype(F32), -1, keepdims=True) / width

    def input_back(i, tick, mean, b):
        r = RN[tick][:, 0:1]
        dn = nn(DM[...], WT[:, cols(b)]).astype(BF).astype(F32)
        xn = SB[tick, :, cols(b)].astype(F32) * r
        PP[i, :, cols(b)] = (r * (dn - xn * mean)).astype(BF)
        for c in send_out(i, b):
            c.start()

    saved.wait()
    for tick in range(2):
        x = chosen(tick, ST[0], ST[1]).astype(BF)
        SB[tick] = x
        xn, r = norm(x)
        XN[(1 + tick) * rows : (2 + tick) * rows, :] = xn
        RN[tick] = jnp.broadcast_to(r, (rows, HS))
    for n in range(PARTS):
        relay(0, n)
    for n in range(PARTS, 2 * PARTS):
        start_own(n)
    pl.when(s > 0)(lambda: gather_start(0, sent_hop, X1, everything))
    pl.when(s < ns - 1)(lambda: gather_start(2, ret_hop, G1, everything))
    for j in range(1, ny - 1):
        for n in range(PARTS):
            relay(j, n)
    pl.when(s > 0)(lambda: gather_finish(0, X1, everything))
    pl.when(s < ns - 1)(lambda: gather_finish(2, G1, everything))

    @pl.when(first)
    def _():
        for c in fresh_in:
            c.wait()

    @pl.when(last)
    def _():
        for c in loss_in:
            c.wait()

    XN[0:rows, :] = norm(X1[...])[0]
    between = jnp.logical_and(y > 0, y < ny - 1)

    out_pieces = range(PARTS, 2 * PARTS)

    @pl.when(between)
    def _():
        for j in range(ny - 1):
            for n in out_pieces:
                relay(j, n)
        for n in out_pieces:
            for j in range(ny - 1):
                from_sibling(j, n)

    own_q.wait()
    for n in range(PARTS):
        own_from_sibling(n)
        for j in range(ny - 1):
            from_sibling(j, n)
    project(0, 3 * rows, XN)
    attend(0, allowed(fr_in[0:1]))
    for tick in range(2):
        ok = allowed(chosen(tick, fr_in[0:1], fr_in[1:2]))
        for k in range(kh):
            PR[tick, k] = probs((1 + tick) * rows, k, ok)

    def turn(b, carry):
        for c in range(0, wide, HS):
            at = pl.ds(pl.multiple_of(b * wide + c, HS), HS)
            WT[:, at] = WQ[at, :].T
        return carry

    lax.fori_loop(0, ny, turn, 0)

    def block(i):
        return jnp.where(y < ny // 2, i, ny - 1 - i)

    def reduce_down(b):
        reduced(0, X1, b)
        pl.when(s < ns - 1)(lambda: hop_down(1, SL.at[0], b).start())

    for i in range(ny):
        if i == 0:
            own_o.wait()
            for n in out_pieces:
                own_from_sibling(n)
        else:

            @pl.when(jnp.logical_not(between))
            def _():
                for n in out_pieces:
                    relay(i - 1, n)
                for n in out_pieces:
                    from_sibling(i - 1, n)

        b = block(i)
        output(0, b)
        part = nn(G1[:, cols(b)], WO[cols(b), :])
        DA[...] = part if i == 0 else DA[...] + part
        if i >= 2:
            reduce_down(block(i - 2))
    mean = heads_back(0, DA[...].astype(BF))
    for b in range(ny):
        input_back(2, 0, mean, b)
    for i in range(ny - 2, ny):
        reduce_down(block(i))

    for i in range(ny):
        b = block(i)
        pl.when(s > 0)(lambda: gather_start(1, hop_down(1, SL.at[0], b), X2, cols(b), b))
    for b in range(ny):
        reduced(2, G1, b)
        pl.when(s > 0)(lambda: hop_up(3, SL.at[2], b).start())
    for b in range(ny):
        pl.when(s < ns - 1)(lambda: gather_start(3, hop_up(3, SL.at[2], b), G2, cols(b), b))
    squares = jnp.zeros((rows, 1), F32)
    mixed = jnp.zeros((rows, WQ.shape[1]), F32)
    for i in range(ny):
        b = block(i)
        pl.when(s > 0)(lambda: gather_finish(1, X2, cols(b), b))
        x = X2[:, cols(b)]
        mixed = mixed + nn(x, WQ[cols(b), :])
        squares = squares + jnp.sum(x.astype(F32) * x.astype(F32), -1, keepdims=True)
    MX[0:rows, :] = (mixed * lax.rsqrt(squares / width + 1e-05)).astype(BF)
    attend(0, allowed(fr_in[1:2]))
    for b in range(ny):
        output(1, b)
    dctx = jnp.zeros((rows, qh * HS), F32)
    for b in range(ny):
        pl.when(s < ns - 1)(lambda: gather_finish(3, G2, cols(b), b))
        dctx = dctx + nn(G2[:, cols(b)], WO[cols(b), :])
    mean = heads_back(1, dctx.astype(BF))

    def finished(i, ag, base, out, b):
        reduced(i, base, b)
        for c in spread(ag, SL.at[i], out.at[0], cols(b), b):
            c.start()

    for b in range(ny):
        input_back(3, 1, mean, b)
        if b % 2:
            finished(1, 4, X2, out_f, b - 1)
            finished(1, 4, X2, out_f, b)
    keep_f = pltpu.make_async_copy(SL.at[1], out_f.at[0, mine], loc_sem.at[7])
    keep_f.start()
    for b in range(ny):
        finished(3, 5, G2, out_b, b)
    keep_b = pltpu.make_async_copy(SL.at[3], out_b.at[0, mine], loc_sem.at[8])
    keep_b.start()

    for n in range(2 * PARTS):
        finish_own(n)
        for j in range(ny - 1):
            finish_line(j, n)
    pl.when(s < ns - 1)(lambda: sent_hop.wait_send())
    pl.when(s > 0)(lambda: ret_hop.wait_send())
    pl.when(s > 0)(lambda: gather_sent(0, X1, everything))
    pl.when(s < ns - 1)(lambda: gather_sent(2, G1, everything))
    for b in range(ny):
        for i in range(4):
            for c in send_out(i, b):
                c.wait_send()
        pl.when(s < ns - 1)(lambda: hop_down(1, SL.at[0], b).wait_send())
        pl.when(s > 0)(lambda: hop_up(3, SL.at[2], b).wait_send())
        pl.when(s > 0)(lambda: gather_sent(1, X2, cols(b), b))
        pl.when(s < ns - 1)(lambda: gather_sent(3, G2, cols(b), b))
    for i, ag, out in ((1, 4, out_f), (3, 5, out_b)):
        for b in range(ny):
            for c in spread_in(ag, out.at[0], cols(b), b):
                c.wait_recv()
            for c in spread(ag, SL.at[i], out.at[0], cols(b), b):
                c.wait_send()
    keep_f.wait()
    keep_b.wait()


def body(fresh, sent, stash, returned, loss_grads, plan, frame_ids, qkv_weight, out_weight):
    nt_ = lax.axis_size("tensor")
    n_fsdp = lax.axis_size("fsdp")
    ny = n_fsdp // 2
    _, rows, width = sent.shape
    depth, columns = qkv_weight.shape[1:]
    inner = out_weight.shape[2]
    kh = (columns - inner) // (2 * HS)
    group = inner // HS // kh
    cut = rows // nt_
    dma = pltpu.SemaphoreType.DMA
    anywhere = pl.BlockSpec(memory_space=pl.ANY)
    whole = pl.BlockSpec(memory_space=pltpu.VMEM)
    act = pltpu.VMEM((rows, width), BF)
    acts = pltpu.VMEM((2, rows, width), BF)
    return pl.pallas_call(
        kernel,
        out_shape=[jax.ShapeDtypeStruct(sent.shape, BF)] * 2,
        in_specs=[anywhere] * 5 + [pl.BlockSpec(memory_space=pltpu.SMEM), whole] + [anywhere] * 2,
        out_specs=[anywhere] * 2,
        scratch_shapes=[
            pltpu.VMEM((n_fsdp * depth, columns), BF),
            pltpu.VMEM((n_fsdp * depth, inner), BF),
            pltpu.VMEM((columns, n_fsdp * depth), BF),
            act, act, acts, acts, act, act,
            pltpu.VMEM((3 * rows, width), BF),
            pltpu.VMEM((2, rows, HS), F32),
            pltpu.VMEM((3 * rows, columns), BF),
            pltpu.VMEM((2, kh, group * rows, rows), F32),
            pltpu.VMEM((rows, inner), BF),
            pltpu.VMEM((rows, columns), BF),
            pltpu.VMEM((rows, inner), F32),
            pltpu.VMEM((4, rows, width), BF),
            pltpu.VMEM((4, nt_ - 1, cut, width), BF),
            pltpu.VMEM((4, cut, width), BF),
            pltpu.VMEM((4, cut, width), BF),
            dma((3, 2 * PARTS)),
            dma((2, ny - 1, 2 * PARTS)),
            dma((2, ny - 1, 2 * PARTS)),
            dma((2, ny - 1, 2 * PARTS)),
            dma((2, ny, 2 * PARTS)),
            dma((9,)),
            dma((4, ny)),
            dma((4, ny)),
            dma((6, nt_ - 1, ny)),
            dma((6, nt_ - 1, ny)),
            dma((4, nt_ - 1, ny)),
            dma((4, nt_ - 1, ny)),
        ],
        compiler_params=pltpu.CompilerParams(
            collective_id=0, has_side_effects=True, vmem_limit_bytes=60 << 20
        ),
        name="relay",
    )(fresh, sent, stash, returned, loss_grads, plan, frame_ids, qkv_weight, out_weight)


def solution(mesh):
    placed = (
        P(None, "fsdp", None),
        P("section", "fsdp", None),
        P("section", None, "fsdp", None),
        P("section", "fsdp", None),
        P(None, "fsdp", None),
        P("section", None),
        P(None, "fsdp"),
        P("section", "fsdp", "tensor"),
        P("section", "fsdp", "tensor"),
    )
    return jax.shard_map(
        body,
        mesh=mesh,
        in_specs=placed,
        out_specs=(P("section", "fsdp", None), P("section", "fsdp", None)),
        check_vma=False,
    )
```

```python
import jax
import jax.numpy as jnp
from jax import lax
from jax.experimental import pallas as pl
from jax.experimental.pallas import tpu as pltpu
from jax.sharding import PartitionSpec as P

HS = 128
MESH = pl.DeviceIdType.MESH
BF = jnp.bfloat16
F32 = jnp.float32
PARTS = 2
WIDE = 512


def nn(a, b):
    return jnp.dot(a, b, preferred_element_type=F32)


def nt(a, b):
    return lax.dot_general(a, b, (((1,), (1,)), ((), ())), preferred_element_type=F32)


def tn(a, b):
    return lax.dot_general(a, b, (((0,), (0,)), ((), ())), preferred_element_type=F32)


def kernel(
    fresh, sent, stash, returned, loss, plan, frames, wq, wo, out_f, out_b,
    WQ, WO, WT, X1, G1, S1, X2, G2, S2, ST, FG, XN, RN, MX, PR, CT, DM, DA, PP1, RB1, SL1, HOP1, PP2, RB2, SL2, HOP2,
    own_sem, line_send, line_recv, sib_send, sib_recv, loc_sem, guest_send, guest_recv, hop1_send, hop1_recv,
    hop2_send, hop2_recv, ag_send, ag_recv, rs_send, rs_recv,
):
    s = lax.axis_index("section")
    f = lax.axis_index("fsdp")
    t = lax.axis_index("tensor")
    ns, nt_ = lax.axis_size("section"), lax.axis_size("tensor")
    ny = lax.axis_size("fsdp") // 2
    y, core = f // 2, lax.rem(f, 2)
    sibling = 2 * y + 1 - core
    rows, width = X2.shape
    cut = rows // nt_
    depth = wq.shape[1]
    piece = depth // PARTS
    qh = WO.shape[1] // HS
    kh = (WQ.shape[1] // HS - qh) // 2
    group = qh // kh
    scale = HS**-0.5
    first, last = s == 0, s == ns - 1
    mine = pl.ds(pl.multiple_of(t * cut, cut), cut)
    wide = width // ny
    between = jnp.logical_and(y > 0, y < ny - 1)
    end = jnp.logical_not(between)
    partner = jnp.where(jnp.logical_xor(y < ny // 2, between), f + 2, f - 2)
    above, below = jnp.minimum(s + 1, ns - 1), jnp.maximum(s - 1, 0)

    def cols(b):
        return pl.ds(pl.multiple_of(b * wide, 128), wide)

    def remote(src, dst, ss, rs, **where):
        return pltpu.make_async_remote_copy(
            src_ref=src, dst_ref=dst, send_sem=ss, recv_sem=rs, device_id=where, device_id_type=MESH
        )

    def also(a, b):
        return jnp.logical_and(a, b)

    barrier = pltpu.get_barrier_semaphore()

    def greet(**where):
        pl.semaphore_signal(barrier, inc=1, device_id=where, device_id_type=MESH)

    greet(fsdp=sibling)
    for k in range(1, nt_):
        greet(tensor=lax.rem(t + k, nt_))
    pl.when(y > 0)(lambda: greet(fsdp=f - 2))
    pl.when(y < ny - 1)(lambda: greet(fsdp=f + 2))
    for inside, place in ((s > 0, s - 1), (s < ns - 1, s + 1)):
        pl.when(inside)(lambda: greet(section=place, fsdp=partner))
        pl.when(also(inside, between))(lambda: greet(section=place))
    neighbours = jnp.where(s > 0, 1, 0) + jnp.where(s < ns - 1, 1, 0)
    partners = nt_ + jnp.where(y > 0, 1, 0) + jnp.where(y < ny - 1, 1, 0)
    partners = partners + neighbours + neighbours * jnp.where(between, 1, 0)
    pl.semaphore_wait(barrier, partners)

    def home(block, n):
        here, there = (wq, WQ) if n < PARTS else (wo, WO)
        at = (n % PARTS) * piece
        row = pl.multiple_of((2 * block + core) * depth + at, 16)
        return here.at[0, pl.ds(at, piece)], there.at[pl.ds(row, piece)]

    def far(block, n):
        there = WQ if n < PARTS else WO
        row = pl.multiple_of((2 * block + 1 - core) * depth + (n % PARTS) * piece, 16)
        return there.at[pl.ds(row, piece)]

    def own_sends(n):
        here, there = home(y, n)
        up = remote(here, there, own_sem.at[0, n], line_recv.at[0, 0, n], fsdp=jnp.minimum(f + 2, 2 * ny - 1))
        down = remote(here, there, own_sem.at[1, n], line_recv.at[1, 0, n], fsdp=jnp.maximum(f - 2, 0))
        over = remote(here, there, own_sem.at[2, n], sib_recv.at[0, ny - 1, n], fsdp=sibling)
        return up, down, over

    def start_own(n):
        up, down, over = own_sends(n)
        pl.when(y < ny - 1)(lambda: up.start())
        pl.when(y > 0)(lambda: down.start())
        over.start()

    def finish_own(n):
        up, down, over = own_sends(n)
        pl.when(y < ny - 1)(lambda: up.wait_send())
        pl.when(y > 0)(lambda: down.wait_send())
        over.wait_send()

    def line(d, j, n):
        block = y - 1 - j if d == 0 else y + 1 + j
        valid = block >= 0 if d == 0 else block <= ny - 1
        goes_on = jnp.logical_and(valid, y < ny - 1 if d == 0 else y > 0)
        block = jnp.clip(block, 0, ny - 1)
        there = home(block, n)[1]
        onward = jnp.clip(f + (2 if d == 0 else -2), 0, 2 * ny - 1)
        nxt = None
        if j < ny - 2:
            nxt = remote(there, there, line_send.at[d, j, n], line_recv.at[d, j + 1, n], fsdp=onward)
        got = remote(there, there, line_send.at[d, j, n], line_recv.at[d, j, n], fsdp=sibling)
        over = remote(there, there, sib_send.at[d, j, n], sib_recv.at[d, j, n], fsdp=sibling)
        other = far(block, n)
        sib = remote(other, other, sib_send.at[d, j, n], sib_recv.at[d, j, n], fsdp=sibling)
        return valid, goes_on, got, nxt, over, sib

    def relay(j, n):
        for d in range(2):
            valid, goes_on, got, nxt, over, _ = line(d, j, n)

            @pl.when(valid)
            def _():
                got.wait_recv()

            if nxt is not None:
                pl.when(goes_on)(lambda: nxt.start())
            pl.when(valid)(lambda: over.start())

    def finish_line(j, n):
        for d in range(2):
            valid, goes_on, _, nxt, over, _ = line(d, j, n)
            if nxt is not None:
                pl.when(goes_on)(lambda: nxt.wait_send())
            pl.when(valid)(lambda: over.wait_send())

    def own_from_sibling(n):
        other = far(y, n)
        remote(other, other, own_sem.at[2, n], sib_recv.at[0, ny - 1, n], fsdp=sibling).wait_recv()

    def from_sibling(j, n):
        for d in range(2):
            valid, _, _, _, _, sib = line(d, j, n)
            pl.when(valid)(lambda: sib.wait_recv())

    for n in range(PARTS):
        start_own(n)

    own_q = pltpu.make_async_copy(wq.at[0], WQ.at[pl.ds(pl.multiple_of(f * depth, 16), depth)], loc_sem.at[0])
    own_o = pltpu.make_async_copy(wo.at[0], WO.at[pl.ds(pl.multiple_of(f * depth, 16), depth)], loc_sem.at[1])
    saved = pltpu.make_async_copy(stash.at[0], ST, loc_sem.at[2])
    saved.start()

    def hop1(i, g):
        src = (sent, returned)[i].at[0, mine]
        place = (above, below)[i]
        to = partner if g else f
        return remote(src, HOP1.at[i, g], hop1_send.at[i], hop1_recv.at[i, g], section=place, fsdp=to)

    goes = (s < ns - 1, s > 0)
    comes = (s > 0, s < ns - 1)
    edge = (first, last)
    for i in range(2):
        pl.when(also(goes[i], between))(lambda: hop1(i, 0).start())
        pl.when(also(goes[i], end))(lambda: hop1(i, 1).start())

    first_in = (X1, G1)
    second_in = (X2, G2)
    at_hand = (fresh, loss)
    own_in = [pltpu.make_async_copy(at_hand[i].at[0], first_in[i].at[0], loc_sem.at[3 + i]) for i in range(2)]
    own_in2 = [pltpu.make_async_copy(at_hand[i].at[1], second_in[i], loc_sem.at[5 + i]) for i in range(2)]
    guest_in = [
        remote(at_hand[i].at[0], first_in[i].at[1], guest_send.at[i], guest_recv.at[i], fsdp=partner) for i in range(2)
    ]
    guest_stash = remote(S1.at[0], S1.at[1], guest_send.at[2], guest_recv.at[2], fsdp=partner)
    guest_frames = remote(frames, FG, guest_send.at[3], guest_recv.at[3], fsdp=partner)
    for i in range(2):
        pl.when(also(edge[i], between))(lambda: own_in[i].start())
        pl.when(also(edge[i], end))(lambda: guest_in[i].start())
        pl.when(edge[i])(lambda: own_in2[i].start())
    pl.when(end)(lambda: guest_frames.start())
    own_q.start()
    own_o.start()

    far_first = sorted(range(1, nt_), key=lambda k: -min(k, nt_ - k))

    def peer(k):
        return lax.rem(t + k, nt_)

    def part_of(k):
        return pl.ds(pl.multiple_of(lax.rem(t + k, nt_) * cut, cut), cut)

    def spread1(i):
        return [
            remote(HOP1.at[i], first_in[i].at[:, mine], ag_send.at[i, k - 1, 0], ag_recv.at[i, k - 1, 0], tensor=peer(k))
            for k in far_first
        ]

    def spread1_in(i):
        copies = []
        for k in far_first:
            there = first_in[i].at[:, part_of(nt_ - k)]
            copies.append(remote(there, there, ag_send.at[i, k - 1, 0], ag_recv.at[i, k - 1, 0], tensor=peer(k)))
        return copies

    def spread(i, src, dst, b):
        at = cols(b)
        return [
            remote(src.at[:, at], dst.at[mine, at], ag_send.at[i, k - 1, b], ag_recv.at[i, k - 1, b], tensor=peer(k))
            for k in far_first
        ]

    def spread_in(i, dst, b):
        copies = []
        for k in far_first:
            there = dst.at[part_of(nt_ - k), cols(b)]
            copies.append(remote(there, there, ag_send.at[i, k - 1, b], ag_recv.at[i, k - 1, b], tensor=peer(k)))
        return copies

    def hop2(i, g, b):
        place = (above, below)[i]
        to = partner if g else f
        return remote(
            SL1.at[i, g, :, cols(b)], HOP2.at[i, :, cols(b)], hop2_send.at[i, g, b], hop2_recv.at[i, b], section=place, fsdp=to
        )

    def gather2(i, b):
        hop2(i, 0, b).wait_recv()
        for c in spread(2 + i, HOP2.at[i], second_in[i], b):
            c.start()
        second_in[i][mine, cols(b)] = HOP2[i, :, cols(b)]

    def gathered2(i, b):
        for c in spread_in(2 + i, second_in[i], b):
            c.wait_recv()

    def norm(x):
        xf = x.astype(F32)
        r = lax.rsqrt(jnp.mean(xf * xf, -1, keepdims=True) + 1e-05)
        return (xf * r).astype(BF), r

    def allowed(fr):
        fr = jnp.broadcast_to(fr, (rows, rows))
        ok = jnp.where(fr <= fr.T, 1.0, 0.0)
        return jnp.concatenate([ok] * group, axis=0) > 0.5

    def chosen(tick, a, b):
        w = plan[0, tick].astype(F32)
        return a.astype(F32) * (1.0 - w) + b.astype(F32) * w

    def project(m0, m1):
        def block(i, carry):
            at = pl.ds(pl.multiple_of(i * WIDE, 128), WIDE)
            MX[m0:m1, at] = nn(XN[m0:m1, :], WQ[:, at]).astype(BF)
            return carry

        lax.fori_loop(0, WQ.shape[1] // WIDE, block, 0)

    fw, b1, b2 = (0, rows), (2 * rows, 3 * rows), 4 * rows

    def heads(m0, first_head):
        return jnp.concatenate(
            [MX[m0 : m0 + rows, (first_head + g) * HS : (first_head + g + 1) * HS] for g in range(group)], axis=0
        )

    def probs(m0, k, ok):
        key = MX[m0 : m0 + rows, (qh + k) * HS : (qh + k + 1) * HS]
        w = jnp.where(ok, jnp.exp(nt(heads(m0, k * group), key) * scale), 0.0)
        return w / jnp.sum(w, -1, keepdims=True)

    def attend(m0, ok):
        for k in range(kh):
            p = probs(m0, k, ok).astype(BF)
            ctx = nn(p, MX[m0 : m0 + rows, (qh + kh + k) * HS : (qh + kh + k + 1) * HS]).astype(BF)
            for g in range(group):
                CT[m0 : m0 + rows, (k * group + g) * HS : (k * group + g + 1) * HS] = ctx[g * rows : (g + 1) * rows]

    def keep_probs(slot, m0, ok):
        for k in range(kh):
            PR[slot, k] = probs(m0, k, ok)

    def send1(i, b):
        return [
            remote(
                PP1.at[i, :, part_of(k), cols(b)], RB1.at[i, k - 1, :, :, cols(b)],
                rs_send.at[i, k - 1, b], rs_recv.at[i, k - 1, b], tensor=peer(k),
            )
            for k in far_first
        ]

    def send2(i, b):
        return [
            remote(
                PP2.at[i, part_of(k), cols(b)], RB2.at[i, k - 1, :, cols(b)],
                rs_send.at[2 + i, k - 1, b], rs_recv.at[2 + i, k - 1, b], tensor=peer(k),
            )
            for k in far_first
        ]

    def reduced1(i, b):
        for c in send1(i, b):
            c.wait_recv()
        for g in range(2):
            total = PP1[i, g, mine, cols(b)].astype(F32)
            for k in range(1, nt_):
                total = total + RB1[i, k - 1, g, :, cols(b)].astype(F32)
            SL1[i, g, :, cols(b)] = (first_in[i][g, mine, cols(b)].astype(F32) + total).astype(BF)
        for g in (1, 0):
            pl.when(goes[i])(lambda: hop2(i, g, b).start())

    def reduced2(i, b):
        for c in send2(i, b):
            c.wait_recv()
        total = PP2[i, mine, cols(b)].astype(F32)
        for k in range(1, nt_):
            total = total + RB2[i, k - 1, :, cols(b)].astype(F32)
        SL2[i, :, cols(b)] = (second_in[i][mine, cols(b)].astype(F32) + total).astype(BF)
        for c in spread(4 + i, SL2.at[i], (out_f, out_b)[i].at[0], b):
            c.start()

    def heads_back(slot, m0, d0, dc):
        for k in range(kh):
            value = MX[m0 : m0 + rows, (qh + kh + k) * HS : (qh + kh + k + 1) * HS]
            key = MX[m0 : m0 + rows, (qh + k) * HS : (qh + k + 1) * HS]
            q = heads(m0, k * group)
            dctx = jnp.concatenate(
                [dc[:, (k * group + g) * HS : (k * group + g + 1) * HS] for g in range(group)], axis=0
            )
            p = PR[slot, k]
            dp = nt(dctx, value).astype(BF).astype(F32)
            ds = (p * (dp - jnp.sum(dp * p, -1, keepdims=True)) * scale).astype(BF)
            dq = nn(ds, key).astype(BF)
            dk = tn(ds, q).astype(BF)
            dv = tn(p.astype(BF), dctx).astype(BF)
            for g in range(group):
                DM[d0 : d0 + rows, (k * group + g) * HS : (k * group + g + 1) * HS] = dq[g * rows : (g + 1) * rows]
            DM[d0 : d0 + rows, (qh + k) * HS : (qh + k + 1) * HS] = dk
            DM[d0 : d0 + rows, (qh + kh + k) * HS : (qh + kh + k + 1) * HS] = dv
        return (
            jnp.sum(DM[d0 : d0 + rows, :].astype(F32) * MX[m0 : m0 + rows, :].astype(F32), -1, keepdims=True) / width
        )

    def norm_back(slot, dn, x, mean):
        r = RN[slot][:, 0:1]
        return (r * (dn.astype(BF).astype(F32) - x.astype(F32) * r * mean)).astype(BF)

    def turn(b, carry):
        for c in range(0, wide, HS):
            at = pl.ds(pl.multiple_of(b * wide + c, HS), HS)
            WT[:, at] = WQ[at, :].T
        return carry

    def turn_all():
        lax.fori_loop(0, ny, turn, 0)

    in_pieces = range(PARTS)
    out_pieces = range(PARTS, 2 * PARTS)

    def prepare(slot, m0, x):
        xn, r = norm(x)
        XN[m0 : m0 + rows, :] = xn
        RN[slot] = jnp.broadcast_to(r, (rows, HS))

    saved.wait()
    S1[0] = chosen(0, ST[0], ST[1]).astype(BF)
    pl.when(end)(lambda: guest_stash.start())
    x = chosen(1, ST[0], ST[1]).astype(BF)
    S2[...] = x
    prepare(2, b2, x)
    for n in in_pieces:
        relay(0, n)
    for n in out_pieces:
        start_own(n)

    @pl.when(between)
    def _():
        for i in range(2):

            @pl.when(comes[i])
            def _():
                for g in range(2):
                    hop1(i, g).wait_recv()
                for c in spread1(i):
                    c.start()
                for g in range(2):
                    first_in[i][g, mine, :] = HOP1[i, g]

        prepare(0, b1[0], S1[0])

    for j in range(1, ny - 1):
        for n in in_pieces:
            relay(j, n)

    @pl.when(between)
    def _():
        for i in range(2):

            @pl.when(comes[i])
            def _():
                for c in spread1_in(i):
                    c.wait_recv()

            @pl.when(edge[i])
            def _():
                own_in[i].wait()
                guest_in[i].wait_recv()

        guest_stash.wait_recv()
        guest_frames.wait_recv()
        prepare(1, b1[1], S1[1])
        for g in range(2):
            XN[fw[g] : fw[g] + rows, :] = norm(X1[g])[0]

    own_q.wait()
    for n in in_pieces:
        own_from_sibling(n)
        for j in range(ny - 1):
            from_sibling(j, n)
    fr = frames[...].astype(F32)

    def keep_second():
        keep_probs(2, b2, allowed(chosen(1, fr[0:1], fr[1:2])))

    def arrive(i):
        for b in range(ny):
            pl.when(comes[i])(lambda: gather2(i, b))

    def second_forward():
        pl.when(edge[0])(lambda: own_in2[0].wait())
        squares = jnp.zeros((rows, 1), F32)
        mixed = jnp.zeros((rows, WQ.shape[1]), F32)
        for b in range(ny):
            pl.when(comes[0])(lambda: gathered2(0, b))
            x = X2[:, cols(b)]
            mixed = mixed + nn(x, WQ[cols(b), :])
            squares = squares + jnp.sum(x.astype(F32) * x.astype(F32), -1, keepdims=True)
        MX[0:rows, :] = (mixed * lax.rsqrt(squares / width + 1e-05)).astype(BF)
        attend(0, allowed(fr[1:2]))

    @pl.when(end)
    def _():
        project(b2, b2 + rows)
        keep_second()
        turn_all()
        own_o.wait()
        for n in out_pieces:
            own_from_sibling(n)
        for j in range(ny - 2):
            for n in out_pieces:
                relay(j, n)
            for n in out_pieces:
                from_sibling(j, n)
        arrive(0)
        second_forward()
        for n in out_pieces:
            relay(ny - 2, n)
        arrive(1)
        for n in out_pieces:
            from_sibling(ny - 2, n)

    @pl.when(between)
    def _():
        project(0, b2 + rows)
        guest = FG[...].astype(F32)
        marks = (fr, guest)
        for n in out_pieces:
            relay(0, n)
        for g in range(2):
            attend(fw[g], allowed(marks[g][0:1]))
        for g in range(2):
            keep_probs(g, b1[g], allowed(chosen(0, marks[g][0:1], marks[g][1:2])))
        turn_all()
        order = (1, 0, 2, 3)
        for i in range(ny):
            if i == 0:
                own_o.wait()
                for n in out_pieces:
                    own_from_sibling(n)
            elif i == 1:
                for n in out_pieces:
                    from_sibling(0, n)
            elif i == 3:
                for j in range(1, ny - 1):
                    for n in out_pieces:
                        relay(j, n)
                    for n in out_pieces:
                        from_sibling(j, n)
            b = jnp.where(y < ny // 2, order[i], ny - 1 - order[i])
            weight = WO[cols(b), :]
            part = nt(CT[...], weight).astype(BF)
            for g in range(2):
                PP1[0, g, :, cols(b)] = part[g * rows : (g + 1) * rows]
            for c in send1(0, b):
                c.start()
            grad = jnp.concatenate([G1[0, :, cols(b)], G1[1, :, cols(b)]], axis=0)
            part = nn(grad, weight)
            DA[...] = part if i == 0 else DA[...] + part
        mean = [heads_back(g, b1[g], g * rows, DA[g * rows : (g + 1) * rows, :].astype(BF)) for g in range(2)]
        for b in range(ny):
            dn = nn(DM[...], WT[:, cols(b)])
            for g in range(2):
                PP1[1, g, :, cols(b)] = norm_back(g, dn[g * rows : (g + 1) * rows], S1[g, :, cols(b)], mean[g])
            for c in send1(1, b):
                c.start()
        for b in range(ny):
            reduced1(0, b)
        for b in range(ny):
            reduced1(1, b)
        arrive(0)
        keep_second()
        arrive(1)
        second_forward()

    for b in range(ny):
        PP2[0, :, cols(b)] = nt(CT[0:rows, :], WO[cols(b), :]).astype(BF)
        for c in send2(0, b):
            c.start()
    pl.when(edge[1])(lambda: own_in2[1].wait())
    dctx = jnp.zeros((rows, qh * HS), F32)
    for b in range(ny):
        pl.when(comes[1])(lambda: gathered2(1, b))
        dctx = dctx + nn(G2[:, cols(b)], WO[cols(b), :])
    mean = heads_back(2, b2, 0, dctx.astype(BF))
    for b in range(ny):
        PP2[1, :, cols(b)] = norm_back(2, nn(DM[0:rows, :], WT[:, cols(b)]), S2[:, cols(b)], mean)
        for c in send2(1, b):
            c.start()
        if b % 2:
            reduced2(0, b - 1)
            reduced2(0, b)
    keep_f = pltpu.make_async_copy(SL2.at[0], out_f.at[0, mine], loc_sem.at[7])
    keep_f.start()
    for b in range(ny):
        reduced2(1, b)
    keep_b = pltpu.make_async_copy(SL2.at[1], out_b.at[0, mine], loc_sem.at[8])
    keep_b.start()

    for n in range(2 * PARTS):
        finish_own(n)
        for j in range(ny - 1):
            finish_line(j, n)

    @pl.when(end)
    def _():
        guest_stash.wait_send()
        guest_frames.wait_send()

    for i in range(2):
        pl.when(goes[i])(lambda: hop1(i, 0).wait_send())
        pl.when(also(edge[i], end))(lambda: guest_in[i].wait_send())

        @pl.when(between)
        def _():
            @pl.when(comes[i])
            def _():
                for c in spread1(i):
                    c.wait_send()

            for b in range(ny):
                for c in send1(i, b):
                    c.wait_send()
                for g in range(2):
                    pl.when(goes[i])(lambda: hop2(i, g, b).wait_send())

        for b in range(ny):
            for c in send2(i, b):
                c.wait_send()

            @pl.when(comes[i])
            def _():
                for c in spread(2 + i, HOP2.at[i], second_in[i], b):
                    c.wait_send()

    for i, out in ((0, out_f), (1, out_b)):
        for b in range(ny):
            for c in spread_in(4 + i, out.at[0], b):
                c.wait_recv()
            for c in spread(4 + i, SL2.at[i], out.at[0], b):
                c.wait_send()
    keep_f.wait()
    keep_b.wait()


def body(fresh, sent, stash, returned, loss_grads, plan, frame_ids, qkv_weight, out_weight):
    nt_ = lax.axis_size("tensor")
    n_fsdp = lax.axis_size("fsdp")
    ny = n_fsdp // 2
    _, rows, width = sent.shape
    depth, columns = qkv_weight.shape[1:]
    inner = out_weight.shape[2]
    kh = (columns - inner) // (2 * HS)
    group = inner // HS // kh
    cut = rows // nt_
    dma = pltpu.SemaphoreType.DMA
    anywhere = pl.BlockSpec(memory_space=pl.ANY)
    whole = pl.BlockSpec(memory_space=pltpu.VMEM)
    act = pltpu.VMEM((rows, width), BF)
    acts = pltpu.VMEM((2, rows, width), BF)
    return pl.pallas_call(
        kernel,
        out_shape=[jax.ShapeDtypeStruct(sent.shape, BF)] * 2,
        in_specs=[anywhere] * 5 + [pl.BlockSpec(memory_space=pltpu.SMEM), whole] + [anywhere] * 2,
        out_specs=[anywhere] * 2,
        scratch_shapes=[
            pltpu.VMEM((n_fsdp * depth, columns), BF),
            pltpu.VMEM((n_fsdp * depth, inner), BF),
            pltpu.VMEM((columns, n_fsdp * depth), BF),
            acts, acts, acts, act, act, act, acts,
            pltpu.VMEM(frame_ids.shape, jnp.int32),
            pltpu.VMEM((5 * rows, width), BF),
            pltpu.VMEM((3, rows, HS), F32),
            pltpu.VMEM((5 * rows, columns), BF),
            pltpu.VMEM((3, kh, group * rows, rows), F32),
            pltpu.VMEM((2 * rows, inner), BF),
            pltpu.VMEM((2 * rows, columns), BF),
            pltpu.VMEM((2 * rows, inner), F32),
            pltpu.VMEM((2, 2, rows, width), BF),
            pltpu.VMEM((2, nt_ - 1, 2, cut, width), BF),
            pltpu.VMEM((2, 2, cut, width), BF),
            pltpu.VMEM((2, 2, cut, width), BF),
            pltpu.VMEM((2, rows, width), BF),
            pltpu.VMEM((2, nt_ - 1, cut, width), BF),
            pltpu.VMEM((2, cut, width), BF),
            pltpu.VMEM((2, cut, width), BF),
            dma((3, 2 * PARTS)),
            dma((2, ny - 1, 2 * PARTS)),
            dma((2, ny - 1, 2 * PARTS)),
            dma((2, ny - 1, 2 * PARTS)),
            dma((2, ny, 2 * PARTS)),
            dma((9,)),
            dma((4,)),
            dma((4,)),
            dma((2,)),
            dma((2, 2)),
            dma((2, 2, ny)),
            dma((2, ny)),
            dma((6, nt_ - 1, ny)),
            dma((6, nt_ - 1, ny)),
            dma((4, nt_ - 1, ny)),
            dma((4, nt_ - 1, ny)),
        ],
        compiler_params=pltpu.CompilerParams(
            collective_id=0, has_side_effects=True, vmem_limit_bytes=60 << 20
        ),
        name="relay",
    )(fresh, sent, stash, returned, loss_grads, plan, frame_ids, qkv_weight, out_weight)


def solution(mesh):
    placed = (
        P(None, "fsdp", None),
        P("section", "fsdp", None),
        P("section", None, "fsdp", None),
        P("section", "fsdp", None),
        P(None, "fsdp", None),
        P("section", None),
        P(None, "fsdp"),
        P("section", "fsdp", "tensor"),
        P("section", "fsdp", "tensor"),
    )
    return jax.shard_map(
        body,
        mesh=mesh,
        in_specs=placed,
        out_specs=(P("section", "fsdp", None), P("section", "fsdp", None)),
        check_vma=False,
    )
```

```python
import jax
import jax.numpy as jnp
from jax import lax
from jax.experimental import pallas as pl
from jax.experimental.pallas import tpu as pltpu
from jax.sharding import PartitionSpec as P

HS = 128
MESH = pl.DeviceIdType.MESH
BF = jnp.bfloat16
F32 = jnp.float32
PARTS = 2
WIDE = 512


def nn(a, b):
    return jnp.dot(a, b, preferred_element_type=F32)


def nt(a, b):
    return lax.dot_general(a, b, (((1,), (1,)), ((), ())), preferred_element_type=F32)


def tn(a, b):
    return lax.dot_general(a, b, (((0,), (0,)), ((), ())), preferred_element_type=F32)


def kernel(
    fresh, sent, stash, returned, loss, plan, frames, wq, wo, out_f, out_b,
    WQ, WO, WT, X1, G1, S1, X2, G2, S2, ST, FG, XN, RN, MX, PR, CT, DM, DA, PP1, RB1, SL1, HOP1, PP2, RB2, SL2, HOP2,
    own_sem, line_send, line_recv, sib_send, sib_recv, loc_sem, guest_send, guest_recv, hop1_send, hop1_recv,
    hop2_send, hop2_recv, ag_send, ag_recv, rs_send, rs_recv, open_sem,
):
    s = lax.axis_index("section")
    f = lax.axis_index("fsdp")
    t = lax.axis_index("tensor")
    ns, nt_ = lax.axis_size("section"), lax.axis_size("tensor")
    ny = lax.axis_size("fsdp") // 2
    y, core = f // 2, lax.rem(f, 2)
    sibling = 2 * y + 1 - core
    rows, width = X2.shape
    cut = rows // nt_
    depth = wq.shape[1]
    piece = depth // PARTS
    qh = WO.shape[1] // HS
    kh = (WQ.shape[1] // HS - qh) // 2
    group = qh // kh
    scale = HS**-0.5
    first, last = s == 0, s == ns - 1
    mine = pl.ds(pl.multiple_of(t * cut, cut), cut)
    wide = width // ny
    between = jnp.logical_and(y > 0, y < ny - 1)
    end = jnp.logical_not(between)
    partner = jnp.where(jnp.logical_xor(y < ny // 2, between), f + 2, f - 2)
    wrap = s == ns // 2
    above, below = jnp.minimum(s + 1, ns - 1), jnp.maximum(s - 1, 0)

    def cols(b):
        return pl.ds(pl.multiple_of(b * wide, 128), wide)

    def remote(src, dst, ss, rs, **where):
        return pltpu.make_async_remote_copy(
            src_ref=src, dst_ref=dst, send_sem=ss, recv_sem=rs, device_id=where, device_id_type=MESH
        )

    def also(a, b):
        return jnp.logical_and(a, b)

    barrier = pltpu.get_barrier_semaphore()

    def greet(**where):
        pl.semaphore_signal(barrier, inc=1, device_id=where, device_id_type=MESH)

    greet(fsdp=sibling)
    for k in range(1, nt_):
        greet(tensor=lax.rem(t + k, nt_))
    pl.when(y > 0)(lambda: greet(fsdp=f - 2))
    pl.when(y < ny - 1)(lambda: greet(fsdp=f + 2))
    pl.when(s > 0)(lambda: greet(section=s - 1, fsdp=partner))
    pl.when(also(s > 0, between))(lambda: greet(section=s - 1))
    links = jnp.where(between, 2, 1)
    partners = nt_ + jnp.where(y > 0, 1, 0) + jnp.where(y < ny - 1, 1, 0)
    partners = partners + links * jnp.where(s < ns - 1, 1, 0)
    pl.semaphore_wait(barrier, partners)

    def answer(**where):
        pl.semaphore_signal(open_sem, inc=1, device_id=where, device_id_type=MESH)

    pl.when(s < ns - 1)(lambda: answer(section=s + 1, fsdp=partner))
    pl.when(also(s < ns - 1, between))(lambda: answer(section=s + 1))

    def home(block, n):
        here, there = (wq, WQ) if n < PARTS else (wo, WO)
        at = (n % PARTS) * piece
        row = pl.multiple_of((2 * block + core) * depth + at, 16)
        return here.at[0, pl.ds(at, piece)], there.at[pl.ds(row, piece)]

    def far(block, n):
        there = WQ if n < PARTS else WO
        row = pl.multiple_of((2 * block + 1 - core) * depth + (n % PARTS) * piece, 16)
        return there.at[pl.ds(row, piece)]

    def own_sends(n):
        here, there = home(y, n)
        up = remote(here, there, own_sem.at[0, n], line_recv.at[0, 0, n], fsdp=jnp.minimum(f + 2, 2 * ny - 1))
        down = remote(here, there, own_sem.at[1, n], line_recv.at[1, 0, n], fsdp=jnp.maximum(f - 2, 0))
        over = remote(here, there, own_sem.at[2, n], sib_recv.at[0, ny - 1, n], fsdp=sibling)
        return up, down, over

    def start_own(n):
        up, down, over = own_sends(n)
        pl.when(y < ny - 1)(lambda: up.start())
        pl.when(y > 0)(lambda: down.start())
        over.start()

    def finish_own(n):
        up, down, over = own_sends(n)
        pl.when(y < ny - 1)(lambda: up.wait_send())
        pl.when(y > 0)(lambda: down.wait_send())
        over.wait_send()

    def line(d, j, n):
        block = y - 1 - j if d == 0 else y + 1 + j
        valid = block >= 0 if d == 0 else block <= ny - 1
        goes_on = jnp.logical_and(valid, y < ny - 1 if d == 0 else y > 0)
        block = jnp.clip(block, 0, ny - 1)
        there = home(block, n)[1]
        onward = jnp.clip(f + (2 if d == 0 else -2), 0, 2 * ny - 1)
        nxt = None
        if j < ny - 2:
            nxt = remote(there, there, line_send.at[d, j, n], line_recv.at[d, j + 1, n], fsdp=onward)
        got = remote(there, there, line_send.at[d, j, n], line_recv.at[d, j, n], fsdp=sibling)
        over = remote(there, there, sib_send.at[d, j, n], sib_recv.at[d, j, n], fsdp=sibling)
        other = far(block, n)
        sib = remote(other, other, sib_send.at[d, j, n], sib_recv.at[d, j, n], fsdp=sibling)
        return valid, goes_on, got, nxt, over, sib

    def relay(j, n):
        for d in range(2):
            valid, goes_on, got, nxt, over, _ = line(d, j, n)

            @pl.when(valid)
            def _():
                got.wait_recv()

            if nxt is not None:
                pl.when(goes_on)(lambda: nxt.start())
            pl.when(valid)(lambda: over.start())

    def finish_line(j, n):
        for d in range(2):
            valid, goes_on, _, nxt, over, _ = line(d, j, n)
            if nxt is not None:
                pl.when(goes_on)(lambda: nxt.wait_send())
            pl.when(valid)(lambda: over.wait_send())

    def own_from_sibling(n):
        other = far(y, n)
        remote(other, other, own_sem.at[2, n], sib_recv.at[0, ny - 1, n], fsdp=sibling).wait_recv()

    def from_sibling(j, n):
        for d in range(2):
            valid, _, _, _, _, sib = line(d, j, n)
            pl.when(valid)(lambda: sib.wait_recv())

    for n in range(PARTS):
        start_own(n)

    own_q = pltpu.make_async_copy(wq.at[0], WQ.at[pl.ds(pl.multiple_of(f * depth, 16), depth)], loc_sem.at[0])
    own_o = pltpu.make_async_copy(wo.at[0], WO.at[pl.ds(pl.multiple_of(f * depth, 16), depth)], loc_sem.at[1])
    saved = pltpu.make_async_copy(stash.at[0], ST, loc_sem.at[2])
    saved.start()

    def hop1(i, g):
        src = (sent, returned)[i].at[0, mine]
        place = (above, below)[i]
        to = partner if g else f
        return remote(src, HOP1.at[i, g], hop1_send.at[i], hop1_recv.at[i, g], section=place, fsdp=to)

    goes = (s < ns - 1, s > 0)
    comes = (s > 0, s < ns - 1)
    edge = (first, last)
    first_in = (X1, G1)
    second_in = (X2, G2)
    at_hand = (fresh, loss)

    def send_hop1(i):
        pl.when(also(goes[i], between))(lambda: hop1(i, 0).start())
        pl.when(also(goes[i], end))(lambda: hop1(i, 1).start())

    own_in = [pltpu.make_async_copy(at_hand[i].at[0, mine], HOP1.at[i, 0], hop1_recv.at[i, 0]) for i in range(2)]
    own_in2 = [pltpu.make_async_copy(at_hand[i].at[1], second_in[i], loc_sem.at[5 + i]) for i in range(2)]
    guest_in = [
        remote(at_hand[i].at[0, mine], HOP1.at[i, 1], guest_send.at[i], hop1_recv.at[i, 1], fsdp=partner) for i in range(2)
    ]
    guest_stash = remote(S1.at[0], S1.at[1], guest_send.at[2], guest_recv.at[0], fsdp=partner)
    guest_frames = remote(frames, FG, guest_send.at[3], guest_recv.at[1], fsdp=partner)
    send_hop1(0)
    for i in range(2):
        pl.when(also(edge[i], between))(lambda: own_in[i].start())
        pl.when(also(edge[i], end))(lambda: guest_in[i].start())
        pl.when(edge[i])(lambda: own_in2[i].start())
    pl.when(end)(lambda: guest_frames.start())
    own_q.start()
    own_o.start()

    far_first = sorted(range(1, nt_), key=lambda k: -min(k, nt_ - k))

    def peer(k):
        return lax.rem(t + k, nt_)

    def part_of(k):
        return pl.ds(pl.multiple_of(lax.rem(t + k, nt_) * cut, cut), cut)

    def spread1(i):
        return [
            remote(HOP1.at[i], first_in[i].at[:, mine], ag_send.at[i, k - 1, 0], ag_recv.at[i, k - 1, 0], tensor=peer(k))
            for k in far_first
        ]

    def spread1_in(i):
        copies = []
        for k in far_first:
            there = first_in[i].at[:, part_of(nt_ - k)]
            copies.append(remote(there, there, ag_send.at[i, k - 1, 0], ag_recv.at[i, k - 1, 0], tensor=peer(k)))
        return copies

    def spread(i, src, dst, b):
        at = cols(b)
        return [
            remote(src.at[:, at], dst.at[mine, at], ag_send.at[i, k - 1, b], ag_recv.at[i, k - 1, b], tensor=peer(k))
            for k in far_first
        ]

    def spread_in(i, dst, b):
        copies = []
        for k in far_first:
            there = dst.at[part_of(nt_ - k), cols(b)]
            copies.append(remote(there, there, ag_send.at[i, k - 1, b], ag_recv.at[i, k - 1, b], tensor=peer(k)))
        return copies

    def hop2(i, g, b):
        place = (above, below)[i]
        to = partner if g else f
        return remote(
            SL1.at[i, g, :, cols(b)], HOP2.at[i, :, cols(b)], hop2_send.at[i, g, b], hop2_recv.at[i, b], section=place, fsdp=to
        )

    def gather2(i, b):
        hop2(i, 0, b).wait_recv()
        for c in spread(2 + i, HOP2.at[i], second_in[i], b):
            c.start()
        second_in[i][mine, cols(b)] = HOP2[i, :, cols(b)]

    def gathered2(i, b):
        for c in spread_in(2 + i, second_in[i], b):
            c.wait_recv()

    def norm(x):
        xf = x.astype(F32)
        r = lax.rsqrt(jnp.mean(xf * xf, -1, keepdims=True) + 1e-05)
        return (xf * r).astype(BF), r

    def allowed(fr):
        fr = jnp.broadcast_to(fr, (rows, rows))
        ok = jnp.where(fr <= fr.T, 1.0, 0.0)
        return jnp.concatenate([ok] * group, axis=0) > 0.5

    def chosen(tick, a, b):
        w = plan[0, tick].astype(F32)
        return a.astype(F32) * (1.0 - w) + b.astype(F32) * w

    def project(m0, m1):
        def block(i, carry):
            at = pl.ds(pl.multiple_of(i * WIDE, 128), WIDE)
            MX[m0:m1, at] = nn(XN[m0:m1, :], WQ[:, at]).astype(BF)
            return carry

        lax.fori_loop(0, WQ.shape[1] // WIDE, block, 0)

    fw, b1, b2 = (0, rows), (2 * rows, 3 * rows), 4 * rows

    def heads(m0, first_head):
        return jnp.concatenate(
            [MX[m0 : m0 + rows, (first_head + g) * HS : (first_head + g + 1) * HS] for g in range(group)], axis=0
        )

    def probs(m0, k, ok):
        key = MX[m0 : m0 + rows, (qh + k) * HS : (qh + k + 1) * HS]
        w = jnp.where(ok, jnp.exp(nt(heads(m0, k * group), key) * scale), 0.0)
        return w / jnp.sum(w, -1, keepdims=True)

    def attend(m0, ok):
        for k in range(kh):
            p = probs(m0, k, ok).astype(BF)
            ctx = nn(p, MX[m0 : m0 + rows, (qh + kh + k) * HS : (qh + kh + k + 1) * HS]).astype(BF)
            for g in range(group):
                CT[m0 : m0 + rows, (k * group + g) * HS : (k * group + g + 1) * HS] = ctx[g * rows : (g + 1) * rows]

    def keep_probs(slot, m0, ok):
        for k in range(kh):
            PR[slot, k] = probs(m0, k, ok)

    def send1(i, b):
        return [
            remote(
                PP1.at[i, :, part_of(k), cols(b)], RB1.at[i, k - 1, :, :, cols(b)],
                rs_send.at[i, k - 1, b], rs_recv.at[i, k - 1, b], tensor=peer(k),
            )
            for k in far_first
        ]

    def send2(i, b):
        return [
            remote(
                PP2.at[i, part_of(k), cols(b)], RB2.at[i, k - 1, :, cols(b)],
                rs_send.at[2 + i, k - 1, b], rs_recv.at[2 + i, k - 1, b], tensor=peer(k),
            )
            for k in far_first
        ]

    def reduced1(i, b):
        for c in send1(i, b):
            c.wait_recv()
        for g in range(2):
            total = PP1[i, g, mine, cols(b)].astype(F32)
            for k in range(1, nt_):
                total = total + RB1[i, k - 1, g, :, cols(b)].astype(F32)
            SL1[i, g, :, cols(b)] = (first_in[i][g, mine, cols(b)].astype(F32) + total).astype(BF)
        for g in (1, 0):
            pl.when(goes[i])(lambda: hop2(i, g, b).start())

    def reduced2(i, b):
        for c in send2(i, b):
            c.wait_recv()
        total = PP2[i, mine, cols(b)].astype(F32)
        for k in range(1, nt_):
            total = total + RB2[i, k - 1, :, cols(b)].astype(F32)
        SL2[i, :, cols(b)] = (second_in[i][mine, cols(b)].astype(F32) + total).astype(BF)
        for c in spread(4 + i, SL2.at[i], (out_f, out_b)[i].at[0], b):
            c.start()

    def heads_back(slot, m0, d0, dc):
        for k in range(kh):
            value = MX[m0 : m0 + rows, (qh + kh + k) * HS : (qh + kh + k + 1) * HS]
            key = MX[m0 : m0 + rows, (qh + k) * HS : (qh + k + 1) * HS]
            q = heads(m0, k * group)
            dctx = jnp.concatenate(
                [dc[:, (k * group + g) * HS : (k * group + g + 1) * HS] for g in range(group)], axis=0
            )
            p = PR[slot, k]
            dp = nt(dctx, value).astype(BF).astype(F32)
            ds = (p * (dp - jnp.sum(dp * p, -1, keepdims=True)) * scale).astype(BF)
            dq = nn(ds, key).astype(BF)
            dk = tn(ds, q).astype(BF)
            dv = tn(p.astype(BF), dctx).astype(BF)
            for g in range(group):
                DM[d0 : d0 + rows, (k * group + g) * HS : (k * group + g + 1) * HS] = dq[g * rows : (g + 1) * rows]
            DM[d0 : d0 + rows, (qh + k) * HS : (qh + k + 1) * HS] = dk
            DM[d0 : d0 + rows, (qh + kh + k) * HS : (qh + kh + k + 1) * HS] = dv
        return (
            jnp.sum(DM[d0 : d0 + rows, :].astype(F32) * MX[m0 : m0 + rows, :].astype(F32), -1, keepdims=True) / width
        )

    def norm_back(slot, dn, x, mean):
        r = RN[slot][:, 0:1]
        return (r * (dn.astype(BF).astype(F32) - x.astype(F32) * r * mean)).astype(BF)

    def turn(b, carry):
        for c in range(0, wide, HS):
            at = pl.ds(pl.multiple_of(b * wide + c, HS), HS)
            WT[:, at] = WQ[at, :].T
        return carry

    def turn_all():
        lax.fori_loop(0, ny, turn, 0)

    in_pieces = range(PARTS)
    out_pieces = range(PARTS, 2 * PARTS)

    def prepare(slot, m0, x):
        xn, r = norm(x)
        XN[m0 : m0 + rows, :] = xn
        RN[slot] = jnp.broadcast_to(r, (rows, HS))

    saved.wait()
    S1[0] = chosen(0, ST[0], ST[1]).astype(BF)
    pl.when(end)(lambda: guest_stash.start())
    x = chosen(1, ST[0], ST[1]).astype(BF)
    S2[...] = x
    prepare(2, b2, x)
    for n in in_pieces:
        relay(0, n)
    for n in out_pieces:
        start_own(n)

    pl.when(s > 0)(lambda: pl.semaphore_wait(open_sem, links))
    send_hop1(1)

    def arrive1(i):
        for g in range(2):
            hop1(i, g).wait_recv()
        for c in spread1(i):
            c.start()
        for g in range(2):
            first_in[i][g, mine, :] = HOP1[i, g]

    @pl.when(between)
    def _():
        arrive1(0)
        prepare(0, b1[0], S1[0])

    for n in in_pieces:
        relay(1, n)
        if n == 0:
            pl.when(between)(lambda: arrive1(1))

    @pl.when(between)
    def _():
        for n in out_pieces:
            relay(0, n)

    for j in range(2, ny - 1):
        for n in in_pieces:
            relay(j, n)

    @pl.when(between)
    def _():
        for i in range(2):
            for c in spread1_in(i):
                c.wait_recv()

        guest_stash.wait_recv()
        guest_frames.wait_recv()
        prepare(1, b1[1], S1[1])
        for g in range(2):
            XN[fw[g] : fw[g] + rows, :] = norm(X1[g])[0]

    own_q.wait()
    for n in in_pieces:
        own_from_sibling(n)
        for j in range(ny - 1):
            from_sibling(j, n)
    fr = frames[...].astype(F32)

    def keep_second():
        keep_probs(2, b2, allowed(chosen(1, fr[0:1], fr[1:2])))

    def arrive(i):
        for b in range(ny):
            pl.when(comes[i])(lambda: gather2(i, b))

    def second_forward():
        pl.when(edge[0])(lambda: own_in2[0].wait())
        squares = jnp.zeros((rows, 1), F32)
        mixed = jnp.zeros((rows, WQ.shape[1]), F32)
        for b in range(ny):
            pl.when(comes[0])(lambda: gathered2(0, b))
            x = X2[:, cols(b)]
            mixed = mixed + nn(x, WQ[cols(b), :])
            squares = squares + jnp.sum(x.astype(F32) * x.astype(F32), -1, keepdims=True)
        MX[0:rows, :] = (mixed * lax.rsqrt(squares / width + 1e-05)).astype(BF)
        attend(0, allowed(fr[1:2]))

    def block(i):
        return jnp.where(y < ny // 2, i, ny - 1 - i)

    def second_output(i):
        b = block(i)
        PP2[0, :, cols(b)] = nt(CT[0:rows, :], WO[cols(b), :]).astype(BF)
        for c in send2(0, b):
            c.start()

    def second_grad(i):
        b = block(i)
        if i == 0:
            pl.when(edge[1])(lambda: own_in2[1].wait())
        pl.when(comes[1])(lambda: gathered2(1, b))
        part = nn(G2[:, cols(b)], WO[cols(b), :])
        DA[0:rows, :] = part if i == 0 else DA[0:rows, :] + part

    @pl.when(end)
    def _():
        project(b2, b2 + rows)
        keep_second()
        turn_all()
        own_o.wait()
        for n in out_pieces:
            own_from_sibling(n)
        for j in range(ny - 2):
            for n in out_pieces:
                relay(j, n)
            for n in out_pieces:
                from_sibling(j, n)

        @pl.when(jnp.logical_not(wrap))
        def _():
            arrive(0)
            second_forward()
            for i in range(ny - 1):
                second_output(i)
            arrive(1)

        for n in out_pieces:
            relay(ny - 2, n)
        pl.when(wrap)(lambda: arrive(1))
        for i in range(ny - 1):
            second_grad(i)
        for n in out_pieces:
            from_sibling(ny - 2, n)
        pl.when(jnp.logical_not(wrap))(lambda: second_output(ny - 1))
        second_grad(ny - 1)

    @pl.when(between)
    def _():
        project(0, b2 + rows)
        guest = FG[...].astype(F32)
        marks = (fr, guest)
        for g in range(2):
            attend(fw[g], allowed(marks[g][0:1]))
        for g in range(2):
            keep_probs(g, b1[g], allowed(chosen(0, marks[g][0:1], marks[g][1:2])))
        turn_all()
        order = (1, 0, 2, 3)
        for i in range(ny):
            if i == 0:
                own_o.wait()
                for n in out_pieces:
                    own_from_sibling(n)
            elif i == 1:
                for n in out_pieces:
                    from_sibling(0, n)
            elif i == 3:
                for j in range(1, ny - 1):
                    for n in out_pieces:
                        relay(j, n)
                    for n in out_pieces:
                        from_sibling(j, n)
            b = jnp.where(y < ny // 2, order[i], ny - 1 - order[i])
            weight = WO[cols(b), :]
            part = nt(CT[...], weight).astype(BF)
            for g in range(2):
                PP1[0, g, :, cols(b)] = part[g * rows : (g + 1) * rows]
            for c in send1(0, b):
                c.start()
            grad = jnp.concatenate([G1[0, :, cols(b)], G1[1, :, cols(b)]], axis=0)
            part = nn(grad, weight)
            DA[...] = part if i == 0 else DA[...] + part
        mean = [heads_back(g, b1[g], g * rows, DA[g * rows : (g + 1) * rows, :].astype(BF)) for g in range(2)]
        for b in range(ny):
            dn = nn(DM[...], WT[:, cols(b)])
            for g in range(2):
                PP1[1, g, :, cols(b)] = norm_back(g, dn[g * rows : (g + 1) * rows], S1[g, :, cols(b)], mean[g])
            for c in send1(1, b):
                c.start()
        for b in range(ny):
            reduced1(0, b)
        for b in range(ny):
            reduced1(1, b)
        pl.when(jnp.logical_not(wrap))(lambda: arrive(0))
        keep_second()
        arrive(1)

        @pl.when(jnp.logical_not(wrap))
        def _():
            second_forward()
            for i in range(ny):
                second_output(i)

        for i in range(ny):
            second_grad(i)

    def second_heads():
        return heads_back(2, b2, 0, DA[0:rows, :].astype(BF))

    def second_input(mean, b):
        PP2[1, :, cols(b)] = norm_back(2, nn(DM[0:rows, :], WT[:, cols(b)]), S2[:, cols(b)], mean)
        for c in send2(1, b):
            c.start()

    @pl.when(jnp.logical_not(wrap))
    def _():
        mean = second_heads()
        for b in range(ny):
            second_input(mean, b)
            if b % 2:
                reduced2(0, b - 1)
                reduced2(0, b)
        for b in range(ny):
            reduced2(1, b)

    @pl.when(wrap)
    def _():
        arrive(0)
        mean = second_heads()
        for b in range(ny):
            second_input(mean, b)
        second_forward()
        for i in range(ny):
            second_output(i)
        for i in (1, 0):
            for b in range(ny):
                reduced2(i, b)

    keep_f = pltpu.make_async_copy(SL2.at[0], out_f.at[0, mine], loc_sem.at[7])
    keep_b = pltpu.make_async_copy(SL2.at[1], out_b.at[0, mine], loc_sem.at[8])
    keep_f.start()
    keep_b.start()

    for n in range(2 * PARTS):
        finish_own(n)
        for j in range(ny - 1):
            finish_line(j, n)

    @pl.when(end)
    def _():
        guest_stash.wait_send()
        guest_frames.wait_send()

    for i in range(2):
        pl.when(goes[i])(lambda: hop1(i, 0).wait_send())
        pl.when(also(edge[i], end))(lambda: guest_in[i].wait_send())

        @pl.when(between)
        def _():
            for c in spread1(i):
                c.wait_send()

            for b in range(ny):
                for c in send1(i, b):
                    c.wait_send()
                for g in range(2):
                    pl.when(goes[i])(lambda: hop2(i, g, b).wait_send())

        for b in range(ny):
            for c in send2(i, b):
                c.wait_send()

            @pl.when(comes[i])
            def _():
                for c in spread(2 + i, HOP2.at[i], second_in[i], b):
                    c.wait_send()

    for i, out in ((0, out_f), (1, out_b)):
        for b in range(ny):
            for c in spread_in(4 + i, out.at[0], b):
                c.wait_recv()
            for c in spread(4 + i, SL2.at[i], out.at[0], b):
                c.wait_send()
    keep_f.wait()
    keep_b.wait()


def body(fresh, sent, stash, returned, loss_grads, plan, frame_ids, qkv_weight, out_weight):
    nt_ = lax.axis_size("tensor")
    n_fsdp = lax.axis_size("fsdp")
    ny = n_fsdp // 2
    _, rows, width = sent.shape
    depth, columns = qkv_weight.shape[1:]
    inner = out_weight.shape[2]
    kh = (columns - inner) // (2 * HS)
    group = inner // HS // kh
    cut = rows // nt_
    dma = pltpu.SemaphoreType.DMA
    anywhere = pl.BlockSpec(memory_space=pl.ANY)
    whole = pl.BlockSpec(memory_space=pltpu.VMEM)
    act = pltpu.VMEM((rows, width), BF)
    acts = pltpu.VMEM((2, rows, width), BF)
    return pl.pallas_call(
        kernel,
        out_shape=[jax.ShapeDtypeStruct(sent.shape, BF)] * 2,
        in_specs=[anywhere] * 5 + [pl.BlockSpec(memory_space=pltpu.SMEM), whole] + [anywhere] * 2,
        out_specs=[anywhere] * 2,
        scratch_shapes=[
            pltpu.VMEM((n_fsdp * depth, columns), BF),
            pltpu.VMEM((n_fsdp * depth, inner), BF),
            pltpu.VMEM((columns, n_fsdp * depth), BF),
            acts, acts, acts, act, act, act, acts,
            pltpu.VMEM(frame_ids.shape, jnp.int32),
            pltpu.VMEM((5 * rows, width), BF),
            pltpu.VMEM((3, rows, HS), F32),
            pltpu.VMEM((5 * rows, columns), BF),
            pltpu.VMEM((3, kh, group * rows, rows), F32),
            pltpu.VMEM((2 * rows, inner), BF),
            pltpu.VMEM((2 * rows, columns), BF),
            pltpu.VMEM((2 * rows, inner), F32),
            pltpu.VMEM((2, 2, rows, width), BF),
            pltpu.VMEM((2, nt_ - 1, 2, cut, width), BF),
            pltpu.VMEM((2, 2, cut, width), BF),
            pltpu.VMEM((2, 2, cut, width), BF),
            pltpu.VMEM((2, rows, width), BF),
            pltpu.VMEM((2, nt_ - 1, cut, width), BF),
            pltpu.VMEM((2, cut, width), BF),
            pltpu.VMEM((2, cut, width), BF),
            dma((3, 2 * PARTS)),
            dma((2, ny - 1, 2 * PARTS)),
            dma((2, ny - 1, 2 * PARTS)),
            dma((2, ny - 1, 2 * PARTS)),
            dma((2, ny, 2 * PARTS)),
            dma((9,)),
            dma((4,)),
            dma((2,)),
            dma((2,)),
            dma((2, 2)),
            dma((2, 2, ny)),
            dma((2, ny)),
            dma((6, nt_ - 1, ny)),
            dma((6, nt_ - 1, ny)),
            dma((4, nt_ - 1, ny)),
            dma((4, nt_ - 1, ny)),
            pltpu.SemaphoreType.REGULAR,
        ],
        compiler_params=pltpu.CompilerParams(
            collective_id=0, has_side_effects=True, vmem_limit_bytes=60 << 20
        ),
        name="relay",
    )(fresh, sent, stash, returned, loss_grads, plan, frame_ids, qkv_weight, out_weight)


def solution(mesh):
    placed = (
        P(None, "fsdp", None),
        P("section", "fsdp", None),
        P("section", None, "fsdp", None),
        P("section", "fsdp", None),
        P(None, "fsdp", None),
        P("section", None),
        P(None, "fsdp"),
        P("section", "fsdp", "tensor"),
        P("section", "fsdp", "tensor"),
    )
    return jax.shard_map(
        body,
        mesh=mesh,
        in_specs=placed,
        out_specs=(P("section", "fsdp", None), P("section", "fsdp", None)),
        check_vma=False,
    )
```

```python
import jax
import jax.numpy as jnp
from jax import lax
from jax.experimental import pallas as pl
from jax.experimental.pallas import tpu as pltpu
from jax.sharding import PartitionSpec as P

HS = 128
MESH = pl.DeviceIdType.MESH
BF = jnp.bfloat16
F32 = jnp.float32
PARTS = 2
WIDE = 512


def nn(a, b):
    return jnp.dot(a, b, preferred_element_type=F32)


def nt(a, b):
    return lax.dot_general(a, b, (((1,), (1,)), ((), ())), preferred_element_type=F32)


def tn(a, b):
    return lax.dot_general(a, b, (((0,), (0,)), ((), ())), preferred_element_type=F32)


def kernel(
    fresh, sent, stash, returned, loss, plan, frames, wq, wo, out_f, out_b,
    WQ, WO, WT, X1, G1, S1, X2, G2, S2, ST, FG, XN, RN, MX, PR, CT, DM, DA, PP1, RB1, SL1, HOP1, PP2, RB2, SL2, HOP2,
    own_sem, line_send, line_recv, sib_send, sib_recv, loc_sem, guest_send, guest_recv, hop1_send, hop1_recv,
    hop2_send, hop2_recv, ag_send, ag_recv, rs_send, rs_recv, open_sem,
):
    s = lax.axis_index("section")
    f = lax.axis_index("fsdp")
    t = lax.axis_index("tensor")
    ns, nt_ = lax.axis_size("section"), lax.axis_size("tensor")
    ny = lax.axis_size("fsdp") // 2
    y, core = f // 2, lax.rem(f, 2)
    sibling = 2 * y + 1 - core
    rows, width = X2.shape
    cut = rows // nt_
    depth = wq.shape[1]
    piece = depth // PARTS
    qh = WO.shape[1] // HS
    kh = (WQ.shape[1] // HS - qh) // 2
    group = qh // kh
    scale = HS**-0.5
    first, last = s == 0, s == ns - 1
    mine = pl.ds(pl.multiple_of(t * cut, cut), cut)
    wide = width // ny
    between = jnp.logical_and(y > 0, y < ny - 1)
    end = jnp.logical_not(between)
    partner = jnp.where(jnp.logical_xor(y < ny // 2, between), f + 2, f - 2)
    wrap = s == ns // 2
    above, below = jnp.minimum(s + 1, ns - 1), jnp.maximum(s - 1, 0)

    def cols(b):
        return pl.ds(pl.multiple_of(b * wide, 128), wide)

    def remote(src, dst, ss, rs, **where):
        return pltpu.make_async_remote_copy(
            src_ref=src, dst_ref=dst, send_sem=ss, recv_sem=rs, device_id=where, device_id_type=MESH
        )

    def also(a, b):
        return jnp.logical_and(a, b)

    barrier = pltpu.get_barrier_semaphore()

    def greet(**where):
        pl.semaphore_signal(barrier, inc=1, device_id=where, device_id_type=MESH)

    greet(fsdp=sibling)
    for k in range(1, nt_):
        greet(tensor=lax.rem(t + k, nt_))
    pl.when(y > 0)(lambda: greet(fsdp=f - 2))
    pl.when(y < ny - 1)(lambda: greet(fsdp=f + 2))
    pl.when(s > 0)(lambda: greet(section=s - 1, fsdp=partner))
    pl.when(also(s > 0, between))(lambda: greet(section=s - 1))
    links = jnp.where(between, 2, 1)
    partners = nt_ + jnp.where(y > 0, 1, 0) + jnp.where(y < ny - 1, 1, 0)
    partners = partners + links * jnp.where(s < ns - 1, 1, 0)
    pl.semaphore_wait(barrier, partners)

    def answer(**where):
        pl.semaphore_signal(open_sem, inc=1, device_id=where, device_id_type=MESH)

    pl.when(s < ns - 1)(lambda: answer(section=s + 1, fsdp=partner))
    pl.when(also(s < ns - 1, between))(lambda: answer(section=s + 1))

    def home(block, n):
        here, there = (wq, WQ) if n < PARTS else (wo, WO)
        at = (n % PARTS) * piece
        row = pl.multiple_of((2 * block + core) * depth + at, 16)
        return here.at[0, pl.ds(at, piece)], there.at[pl.ds(row, piece)]

    def far(block, n):
        there = WQ if n < PARTS else WO
        row = pl.multiple_of((2 * block + 1 - core) * depth + (n % PARTS) * piece, 16)
        return there.at[pl.ds(row, piece)]

    def own_sends(n):
        here, there = home(y, n)
        up = remote(here, there, own_sem.at[0, n], line_recv.at[0, 0, n], fsdp=jnp.minimum(f + 2, 2 * ny - 1))
        down = remote(here, there, own_sem.at[1, n], line_recv.at[1, 0, n], fsdp=jnp.maximum(f - 2, 0))
        over = remote(here, there, own_sem.at[2, n], sib_recv.at[0, ny - 1, n], fsdp=sibling)
        return up, down, over

    def start_own(n):
        up, down, over = own_sends(n)
        pl.when(y < ny - 1)(lambda: up.start())
        pl.when(y > 0)(lambda: down.start())
        over.start()

    def finish_own(n):
        up, down, over = own_sends(n)
        pl.when(y < ny - 1)(lambda: up.wait_send())
        pl.when(y > 0)(lambda: down.wait_send())
        over.wait_send()

    def line(d, j, n):
        block = y - 1 - j if d == 0 else y + 1 + j
        valid = block >= 0 if d == 0 else block <= ny - 1
        goes_on = jnp.logical_and(valid, y < ny - 1 if d == 0 else y > 0)
        block = jnp.clip(block, 0, ny - 1)
        there = home(block, n)[1]
        onward = jnp.clip(f + (2 if d == 0 else -2), 0, 2 * ny - 1)
        nxt = None
        if j < ny - 2:
            nxt = remote(there, there, line_send.at[d, j, n], line_recv.at[d, j + 1, n], fsdp=onward)
        got = remote(there, there, line_send.at[d, j, n], line_recv.at[d, j, n], fsdp=sibling)
        over = remote(there, there, sib_send.at[d, j, n], sib_recv.at[d, j, n], fsdp=sibling)
        other = far(block, n)
        sib = remote(other, other, sib_send.at[d, j, n], sib_recv.at[d, j, n], fsdp=sibling)
        return valid, goes_on, got, nxt, over, sib

    def relay(j, n):
        for d in range(2):
            valid, goes_on, got, nxt, over, _ = line(d, j, n)

            @pl.when(valid)
            def _():
                got.wait_recv()

            if nxt is not None:
                pl.when(goes_on)(lambda: nxt.start())
            pl.when(valid)(lambda: over.start())

    def finish_line(j, n):
        for d in range(2):
            valid, goes_on, _, nxt, over, _ = line(d, j, n)
            if nxt is not None:
                pl.when(goes_on)(lambda: nxt.wait_send())
            pl.when(valid)(lambda: over.wait_send())

    def own_from_sibling(n):
        other = far(y, n)
        remote(other, other, own_sem.at[2, n], sib_recv.at[0, ny - 1, n], fsdp=sibling).wait_recv()

    def from_sibling(j, n):
        for d in range(2):
            valid, _, _, _, _, sib = line(d, j, n)
            pl.when(valid)(lambda: sib.wait_recv())

    for n in range(PARTS):
        start_own(n)

    own_q = pltpu.make_async_copy(wq.at[0], WQ.at[pl.ds(pl.multiple_of(f * depth, 16), depth)], loc_sem.at[0])
    own_o = pltpu.make_async_copy(wo.at[0], WO.at[pl.ds(pl.multiple_of(f * depth, 16), depth)], loc_sem.at[1])
    saved = pltpu.make_async_copy(stash.at[0], ST, loc_sem.at[2])
    saved.start()

    def hop1(i, g):
        src = (sent, returned)[i].at[0, mine]
        place = (above, below)[i]
        to = partner if g else f
        return remote(src, HOP1.at[i, g], hop1_send.at[i], hop1_recv.at[i, g], section=place, fsdp=to)

    goes = (s < ns - 1, s > 0)
    comes = (s > 0, s < ns - 1)
    edge = (first, last)
    first_in = (X1, G1)
    second_in = (X2, G2)
    at_hand = (fresh, loss)

    def send_hop1(i):
        pl.when(also(goes[i], between))(lambda: hop1(i, 0).start())
        pl.when(also(goes[i], end))(lambda: hop1(i, 1).start())

    own_in = [pltpu.make_async_copy(at_hand[i].at[0, mine], HOP1.at[i, 0], hop1_recv.at[i, 0]) for i in range(2)]
    own_in2 = [pltpu.make_async_copy(at_hand[i].at[1], second_in[i], loc_sem.at[5 + i]) for i in range(2)]
    guest_in = [
        remote(at_hand[i].at[0, mine], HOP1.at[i, 1], guest_send.at[i], hop1_recv.at[i, 1], fsdp=partner) for i in range(2)
    ]
    guest_stash = remote(S1.at[0], S1.at[1], guest_send.at[2], guest_recv.at[0], fsdp=partner)
    guest_frames = remote(frames, FG, guest_send.at[3], guest_recv.at[1], fsdp=partner)
    send_hop1(0)
    for i in range(2):
        pl.when(also(edge[i], between))(lambda: own_in[i].start())
        pl.when(also(edge[i], end))(lambda: guest_in[i].start())
        pl.when(edge[i])(lambda: own_in2[i].start())
    pl.when(end)(lambda: guest_frames.start())
    own_q.start()
    own_o.start()

    far_first = sorted(range(1, nt_), key=lambda k: -min(k, nt_ - k))

    def peer(k):
        return lax.rem(t + k, nt_)

    def part_of(k):
        return pl.ds(pl.multiple_of(lax.rem(t + k, nt_) * cut, cut), cut)

    def spread1(i):
        return [
            remote(HOP1.at[i], first_in[i].at[:, mine], ag_send.at[i, k - 1, 0], ag_recv.at[i, k - 1, 0], tensor=peer(k))
            for k in far_first
        ]

    def spread1_in(i):
        copies = []
        for k in far_first:
            there = first_in[i].at[:, part_of(nt_ - k)]
            copies.append(remote(there, there, ag_send.at[i, k - 1, 0], ag_recv.at[i, k - 1, 0], tensor=peer(k)))
        return copies

    def spread(i, src, dst, b):
        at = cols(b)
        return [
            remote(src.at[:, at], dst.at[mine, at], ag_send.at[i, k - 1, b], ag_recv.at[i, k - 1, b], tensor=peer(k))
            for k in far_first
        ]

    def spread_in(i, dst, b):
        copies = []
        for k in far_first:
            there = dst.at[part_of(nt_ - k), cols(b)]
            copies.append(remote(there, there, ag_send.at[i, k - 1, b], ag_recv.at[i, k - 1, b], tensor=peer(k)))
        return copies

    def hop2(i, g, b):
        place = (above, below)[i]
        to = partner if g else f
        return remote(
            SL1.at[i, g, :, cols(b)], HOP2.at[i, :, cols(b)], hop2_send.at[i, g, b], hop2_recv.at[i, b], section=place, fsdp=to
        )

    def gather2(i, b):
        hop2(i, 0, b).wait_recv()
        for c in spread(2 + i, HOP2.at[i], second_in[i], b):
            c.start()
        second_in[i][mine, cols(b)] = HOP2[i, :, cols(b)]

    def gathered2(i, b):
        for c in spread_in(2 + i, second_in[i], b):
            c.wait_recv()

    def norm(x):
        xf = x.astype(F32)
        r = lax.rsqrt(jnp.mean(xf * xf, -1, keepdims=True) + 1e-05)
        return (xf * r).astype(BF), r

    def allowed(fr):
        fr = jnp.broadcast_to(fr, (rows, rows))
        ok = jnp.where(fr <= fr.T, 1.0, 0.0)
        return jnp.concatenate([ok] * group, axis=0) > 0.5

    def chosen(tick, a, b):
        w = plan[0, tick].astype(F32)
        return a.astype(F32) * (1.0 - w) + b.astype(F32) * w

    def project(m0, m1):
        def block(i, carry):
            at = pl.ds(pl.multiple_of(i * WIDE, 128), WIDE)
            MX[m0:m1, at] = nn(XN[m0:m1, :], WQ[:, at]).astype(BF)
            return carry

        lax.fori_loop(0, WQ.shape[1] // WIDE, block, 0)

    fw, b1, b2 = (0, rows), (2 * rows, 3 * rows), 4 * rows

    def heads(m0, first_head):
        return jnp.concatenate(
            [MX[m0 : m0 + rows, (first_head + g) * HS : (first_head + g + 1) * HS] for g in range(group)], axis=0
        )

    def probs(m0, k, ok):
        key = MX[m0 : m0 + rows, (qh + k) * HS : (qh + k + 1) * HS]
        w = jnp.where(ok, jnp.exp(nt(heads(m0, k * group), key) * scale), 0.0)
        return w / jnp.sum(w, -1, keepdims=True)

    def attend(m0, ok):
        for k in range(kh):
            p = probs(m0, k, ok).astype(BF)
            ctx = nn(p, MX[m0 : m0 + rows, (qh + kh + k) * HS : (qh + kh + k + 1) * HS]).astype(BF)
            for g in range(group):
                CT[m0 : m0 + rows, (k * group + g) * HS : (k * group + g + 1) * HS] = ctx[g * rows : (g + 1) * rows]

    def keep_probs(slot, m0, ok):
        for k in range(kh):
            PR[slot, k] = probs(m0, k, ok)

    def send1(i, b):
        return [
            remote(
                PP1.at[i, :, part_of(k), cols(b)], RB1.at[i, k - 1, :, :, cols(b)],
                rs_send.at[i, k - 1, b], rs_recv.at[i, k - 1, b], tensor=peer(k),
            )
            for k in far_first
        ]

    def send2(i, b):
        return [
            remote(
                PP2.at[i, part_of(k), cols(b)], RB2.at[i, k - 1, :, cols(b)],
                rs_send.at[2 + i, k - 1, b], rs_recv.at[2 + i, k - 1, b], tensor=peer(k),
            )
            for k in far_first
        ]

    def reduced1(i, b):
        for c in send1(i, b):
            c.wait_recv()
        for g in range(2):
            total = PP1[i, g, mine, cols(b)].astype(F32)
            for k in range(1, nt_):
                total = total + RB1[i, k - 1, g, :, cols(b)].astype(F32)
            SL1[i, g, :, cols(b)] = (first_in[i][g, mine, cols(b)].astype(F32) + total).astype(BF)
        for g in (1, 0):
            pl.when(goes[i])(lambda: hop2(i, g, b).start())

    def reduced2(i, b):
        for c in send2(i, b):
            c.wait_recv()
        total = PP2[i, mine, cols(b)].astype(F32)
        for k in range(1, nt_):
            total = total + RB2[i, k - 1, :, cols(b)].astype(F32)
        SL2[i, :, cols(b)] = (second_in[i][mine, cols(b)].astype(F32) + total).astype(BF)
        for c in spread(4 + i, SL2.at[i], (out_f, out_b)[i].at[0], b):
            c.start()

    def heads_back(slot, m0, d0, dc):
        for k in range(kh):
            value = MX[m0 : m0 + rows, (qh + kh + k) * HS : (qh + kh + k + 1) * HS]
            key = MX[m0 : m0 + rows, (qh + k) * HS : (qh + k + 1) * HS]
            q = heads(m0, k * group)
            dctx = jnp.concatenate(
                [dc[:, (k * group + g) * HS : (k * group + g + 1) * HS] for g in range(group)], axis=0
            )
            p = PR[slot, k]
            dp = nt(dctx, value).astype(BF).astype(F32)
            ds = (p * (dp - jnp.sum(dp * p, -1, keepdims=True)) * scale).astype(BF)
            dq = nn(ds, key).astype(BF)
            dk = tn(ds, q).astype(BF)
            dv = tn(p.astype(BF), dctx).astype(BF)
            for g in range(group):
                DM[d0 : d0 + rows, (k * group + g) * HS : (k * group + g + 1) * HS] = dq[g * rows : (g + 1) * rows]
            DM[d0 : d0 + rows, (qh + k) * HS : (qh + k + 1) * HS] = dk
            DM[d0 : d0 + rows, (qh + kh + k) * HS : (qh + kh + k + 1) * HS] = dv
        return (
            jnp.sum(DM[d0 : d0 + rows, :].astype(F32) * MX[m0 : m0 + rows, :].astype(F32), -1, keepdims=True) / width
        )

    def norm_back(slot, dn, x, mean):
        r = RN[slot][:, 0:1]
        return (r * (dn.astype(BF).astype(F32) - x.astype(F32) * r * mean)).astype(BF)

    def turn(b, carry):
        for c in range(0, wide, HS):
            at = pl.ds(pl.multiple_of(b * wide + c, HS), HS)
            WT[:, at] = WQ[at, :].T
        return carry

    def turn_all():
        lax.fori_loop(0, ny, turn, 0)

    in_pieces = range(PARTS)
    out_pieces = range(PARTS, 2 * PARTS)

    def prepare(slot, m0, x):
        xn, r = norm(x)
        XN[m0 : m0 + rows, :] = xn
        RN[slot] = jnp.broadcast_to(r, (rows, HS))

    saved.wait()
    S1[0] = chosen(0, ST[0], ST[1]).astype(BF)
    pl.when(end)(lambda: guest_stash.start())
    x = chosen(1, ST[0], ST[1]).astype(BF)
    S2[...] = x
    prepare(2, b2, x)
    for n in in_pieces:
        relay(0, n)
    for n in out_pieces:
        start_own(n)

    pl.when(s > 0)(lambda: pl.semaphore_wait(open_sem, links))
    send_hop1(1)

    def arrive1(i):
        for g in range(2):
            hop1(i, g).wait_recv()
        for c in spread1(i):
            c.start()
        for g in range(2):
            first_in[i][g, mine, :] = HOP1[i, g]

    @pl.when(between)
    def _():
        arrive1(0)
        prepare(0, b1[0], S1[0])

    for n in in_pieces:
        relay(1, n)
        if n == 0:
            pl.when(between)(lambda: arrive1(1))

    @pl.when(between)
    def _():
        for n in out_pieces:
            relay(0, n)

    for j in range(2, ny - 1):
        for n in in_pieces:
            relay(j, n)

    @pl.when(between)
    def _():
        for i in range(2):
            for c in spread1_in(i):
                c.wait_recv()

        guest_stash.wait_recv()
        guest_frames.wait_recv()
        prepare(1, b1[1], S1[1])
        for g in range(2):
            XN[fw[g] : fw[g] + rows, :] = norm(X1[g])[0]

    own_q.wait()
    for n in in_pieces:
        own_from_sibling(n)
        for j in range(ny - 1):
            from_sibling(j, n)
    fr = frames[...].astype(F32)

    def keep_second():
        keep_probs(2, b2, allowed(chosen(1, fr[0:1], fr[1:2])))

    def arrive(i):
        for b in range(ny):
            pl.when(comes[i])(lambda: gather2(i, b))

    def second_forward():
        pl.when(edge[0])(lambda: own_in2[0].wait())
        squares = jnp.zeros((rows, 1), F32)
        mixed = jnp.zeros((rows, WQ.shape[1]), F32)
        for b in range(ny):
            pl.when(comes[0])(lambda: gathered2(0, b))
            x = X2[:, cols(b)]
            mixed = mixed + nn(x, WQ[cols(b), :])
            squares = squares + jnp.sum(x.astype(F32) * x.astype(F32), -1, keepdims=True)
        MX[0:rows, :] = (mixed * lax.rsqrt(squares / width + 1e-05)).astype(BF)
        attend(0, allowed(fr[1:2]))

    def block(i):
        return jnp.where(y < ny // 2, i, ny - 1 - i)

    def second_output(i):
        b = block(i)
        PP2[0, :, cols(b)] = nt(CT[0:rows, :], WO[cols(b), :]).astype(BF)
        for c in send2(0, b):
            c.start()

    def second_grad(i):
        b = block(i)
        if i == 0:
            pl.when(edge[1])(lambda: own_in2[1].wait())
        pl.when(comes[1])(lambda: gathered2(1, b))
        part = nn(G2[:, cols(b)], WO[cols(b), :])
        DA[0:rows, :] = part if i == 0 else DA[0:rows, :] + part

    @pl.when(end)
    def _():
        project(b2, b2 + rows)
        keep_second()
        turn_all()
        own_o.wait()
        for n in out_pieces:
            own_from_sibling(n)
        for j in range(ny - 2):
            for n in out_pieces:
                relay(j, n)
            for n in out_pieces:
                from_sibling(j, n)
        for n in out_pieces[:-1]:
            relay(ny - 2, n)
        pl.when(jnp.logical_not(wrap))(lambda: arrive(0))
        relay(ny - 2, out_pieces[-1])
        arrive(1)
        pl.when(jnp.logical_not(wrap))(second_forward)
        for n in out_pieces:
            from_sibling(ny - 2, n)

        @pl.when(jnp.logical_not(wrap))
        def _():
            for i in range(ny):
                second_output(i)

        for i in range(ny):
            second_grad(i)

    @pl.when(between)
    def _():
        project(0, b2 + rows)
        guest = FG[...].astype(F32)
        marks = (fr, guest)
        for g in range(2):
            attend(fw[g], allowed(marks[g][0:1]))
        for g in range(2):
            keep_probs(g, b1[g], allowed(chosen(0, marks[g][0:1], marks[g][1:2])))
        turn_all()
        order = (1, 0, 2, 3)
        for i in range(ny):
            if i == 0:
                own_o.wait()
                for n in out_pieces:
                    own_from_sibling(n)
            elif i == 1:
                for n in out_pieces:
                    from_sibling(0, n)
            elif i == 3:
                for j in range(1, ny - 1):
                    for n in out_pieces:
                        relay(j, n)
                    for n in out_pieces:
                        from_sibling(j, n)
            b = jnp.where(y < ny // 2, order[i], ny - 1 - order[i])
            weight = WO[cols(b), :]
            part = nt(CT[...], weight).astype(BF)
            for g in range(2):
                PP1[0, g, :, cols(b)] = part[g * rows : (g + 1) * rows]
            for c in send1(0, b):
                c.start()
            grad = jnp.concatenate([G1[0, :, cols(b)], G1[1, :, cols(b)]], axis=0)
            part = nn(grad, weight)
            DA[...] = part if i == 0 else DA[...] + part
        mean = [heads_back(g, b1[g], g * rows, DA[g * rows : (g + 1) * rows, :].astype(BF)) for g in range(2)]
        for b in range(ny):
            dn = nn(DM[...], WT[:, cols(b)])
            for g in range(2):
                PP1[1, g, :, cols(b)] = norm_back(g, dn[g * rows : (g + 1) * rows], S1[g, :, cols(b)], mean[g])
            for c in send1(1, b):
                c.start()
        for b in range(ny):
            reduced1(0, b)
        for b in range(ny):
            reduced1(1, b)
        pl.when(jnp.logical_not(wrap))(lambda: arrive(0))
        keep_second()
        arrive(1)

        @pl.when(jnp.logical_not(wrap))
        def _():
            second_forward()
            for i in range(ny):
                second_output(i)

        for i in range(ny):
            second_grad(i)

    def second_heads():
        return heads_back(2, b2, 0, DA[0:rows, :].astype(BF))

    def second_input(mean, b):
        PP2[1, :, cols(b)] = norm_back(2, nn(DM[0:rows, :], WT[:, cols(b)]), S2[:, cols(b)], mean)
        for c in send2(1, b):
            c.start()

    @pl.when(jnp.logical_not(wrap))
    def _():
        mean = second_heads()
        for b in range(ny):
            second_input(mean, b)
            if b % 2:
                reduced2(0, b - 1)
                reduced2(0, b)
        for b in range(ny):
            reduced2(1, b)

    @pl.when(wrap)
    def _():
        arrive(0)
        mean = second_heads()
        for b in range(ny):
            second_input(mean, b)
        second_forward()
        for i in range(ny):
            second_output(i)
        for i in (1, 0):
            for b in range(ny):
                reduced2(i, b)

    keep_f = pltpu.make_async_copy(SL2.at[0], out_f.at[0, mine], loc_sem.at[7])
    keep_b = pltpu.make_async_copy(SL2.at[1], out_b.at[0, mine], loc_sem.at[8])
    keep_f.start()
    keep_b.start()

    for n in range(2 * PARTS):
        finish_own(n)
        for j in range(ny - 1):
            finish_line(j, n)

    @pl.when(end)
    def _():
        guest_stash.wait_send()
        guest_frames.wait_send()

    for i in range(2):
        pl.when(goes[i])(lambda: hop1(i, 0).wait_send())
        pl.when(also(edge[i], end))(lambda: guest_in[i].wait_send())

        @pl.when(between)
        def _():
            for c in spread1(i):
                c.wait_send()

            for b in range(ny):
                for c in send1(i, b):
                    c.wait_send()
                for g in range(2):
                    pl.when(goes[i])(lambda: hop2(i, g, b).wait_send())

        for b in range(ny):
            for c in send2(i, b):
                c.wait_send()

            @pl.when(comes[i])
            def _():
                for c in spread(2 + i, HOP2.at[i], second_in[i], b):
                    c.wait_send()

    for i, out in ((0, out_f), (1, out_b)):
        for b in range(ny):
            for c in spread_in(4 + i, out.at[0], b):
                c.wait_recv()
            for c in spread(4 + i, SL2.at[i], out.at[0], b):
                c.wait_send()
    keep_f.wait()
    keep_b.wait()


def body(fresh, sent, stash, returned, loss_grads, plan, frame_ids, qkv_weight, out_weight):
    nt_ = lax.axis_size("tensor")
    n_fsdp = lax.axis_size("fsdp")
    ny = n_fsdp // 2
    _, rows, width = sent.shape
    depth, columns = qkv_weight.shape[1:]
    inner = out_weight.shape[2]
    kh = (columns - inner) // (2 * HS)
    group = inner // HS // kh
    cut = rows // nt_
    dma = pltpu.SemaphoreType.DMA
    anywhere = pl.BlockSpec(memory_space=pl.ANY)
    whole = pl.BlockSpec(memory_space=pltpu.VMEM)
    act = pltpu.VMEM((rows, width), BF)
    acts = pltpu.VMEM((2, rows, width), BF)
    return pl.pallas_call(
        kernel,
        out_shape=[jax.ShapeDtypeStruct(sent.shape, BF)] * 2,
        in_specs=[anywhere] * 5 + [pl.BlockSpec(memory_space=pltpu.SMEM), whole] + [anywhere] * 2,
        out_specs=[anywhere] * 2,
        scratch_shapes=[
            pltpu.VMEM((n_fsdp * depth, columns), BF),
            pltpu.VMEM((n_fsdp * depth, inner), BF),
            pltpu.VMEM((columns, n_fsdp * depth), BF),
            acts, acts, acts, act, act, act, acts,
            pltpu.VMEM(frame_ids.shape, jnp.int32),
            pltpu.VMEM((5 * rows, width), BF),
            pltpu.VMEM((3, rows, HS), F32),
            pltpu.VMEM((5 * rows, columns), BF),
            pltpu.VMEM((3, kh, group * rows, rows), F32),
            pltpu.VMEM((2 * rows, inner), BF),
            pltpu.VMEM((2 * rows, columns), BF),
            pltpu.VMEM((2 * rows, inner), F32),
            pltpu.VMEM((2, 2, rows, width), BF),
            pltpu.VMEM((2, nt_ - 1, 2, cut, width), BF),
            pltpu.VMEM((2, 2, cut, width), BF),
            pltpu.VMEM((2, 2, cut, width), BF),
            pltpu.VMEM((2, rows, width), BF),
            pltpu.VMEM((2, nt_ - 1, cut, width), BF),
            pltpu.VMEM((2, cut, width), BF),
            pltpu.VMEM((2, cut, width), BF),
            dma((3, 2 * PARTS)),
            dma((2, ny - 1, 2 * PARTS)),
            dma((2, ny - 1, 2 * PARTS)),
            dma((2, ny - 1, 2 * PARTS)),
            dma((2, ny, 2 * PARTS)),
            dma((9,)),
            dma((4,)),
            dma((2,)),
            dma((2,)),
            dma((2, 2)),
            dma((2, 2, ny)),
            dma((2, ny)),
            dma((6, nt_ - 1, ny)),
            dma((6, nt_ - 1, ny)),
            dma((4, nt_ - 1, ny)),
            dma((4, nt_ - 1, ny)),
            pltpu.SemaphoreType.REGULAR,
        ],
        compiler_params=pltpu.CompilerParams(
            collective_id=0, has_side_effects=True, vmem_limit_bytes=60 << 20
        ),
        name="relay",
    )(fresh, sent, stash, returned, loss_grads, plan, frame_ids, qkv_weight, out_weight)


def solution(mesh):
    placed = (
        P(None, "fsdp", None),
        P("section", "fsdp", None),
        P("section", None, "fsdp", None),
        P("section", "fsdp", None),
        P(None, "fsdp", None),
        P("section", None),
        P(None, "fsdp"),
        P("section", "fsdp", "tensor"),
        P("section", "fsdp", "tensor"),
    )
    return jax.shard_map(
        body,
        mesh=mesh,
        in_specs=placed,
        out_specs=(P("section", "fsdp", None), P("section", "fsdp", None)),
        check_vma=False,
    )
```

```python
import jax
import jax.numpy as jnp
from jax import lax
from jax.experimental import pallas as pl
from jax.experimental.pallas import tpu as pltpu
from jax.sharding import PartitionSpec as P

HS = 128
MESH = pl.DeviceIdType.MESH
BF = jnp.bfloat16
F32 = jnp.float32
PARTS = 2
WIDE = 512


def nn(a, b):
    return jnp.dot(a, b, preferred_element_type=F32)


def nt(a, b):
    return lax.dot_general(a, b, (((1,), (1,)), ((), ())), preferred_element_type=F32)


def tn(a, b):
    return lax.dot_general(a, b, (((0,), (0,)), ((), ())), preferred_element_type=F32)


def kernel(
    fresh, sent, stash, returned, loss, plan, frames, wq, wo, out_f, out_b,
    WQ, WO, WT, X1, G1, S1, X2, G2, S2, ST, FG, XN, RN, MX, PR, CT, DM, DA, PP1, RB1, SL1, HOP1, PP2, RB2, SL2, HOP2,
    own_sem, line_send, line_recv, sib_send, sib_recv, loc_sem, guest_send, guest_recv, hop1_send, hop1_recv,
    hop2_send, hop2_recv, ag_send, ag_recv, rs_send, rs_recv, open_sem,
):
    s = lax.axis_index("section")
    f = lax.axis_index("fsdp")
    t = lax.axis_index("tensor")
    ns, nt_ = lax.axis_size("section"), lax.axis_size("tensor")
    ny = lax.axis_size("fsdp") // 2
    y, core = f // 2, lax.rem(f, 2)
    sibling = 2 * y + 1 - core
    rows, width = X2.shape
    cut = rows // nt_
    depth = wq.shape[1]
    piece = depth // PARTS
    qh = WO.shape[1] // HS
    kh = (WQ.shape[1] // HS - qh) // 2
    group = qh // kh
    scale = HS**-0.5
    first, last = s == 0, s == ns - 1
    mine = pl.ds(pl.multiple_of(t * cut, cut), cut)
    wide = width // ny
    between = jnp.logical_and(y > 0, y < ny - 1)
    end = jnp.logical_not(between)
    partner = jnp.where(jnp.logical_xor(y < ny // 2, between), f + 2, f - 2)
    wrap = s == ns // 2
    above, below = jnp.minimum(s + 1, ns - 1), jnp.maximum(s - 1, 0)

    def cols(b):
        return pl.ds(pl.multiple_of(b * wide, 128), wide)

    def remote(src, dst, ss, rs, **where):
        return pltpu.make_async_remote_copy(
            src_ref=src, dst_ref=dst, send_sem=ss, recv_sem=rs, device_id=where, device_id_type=MESH
        )

    def also(a, b):
        return jnp.logical_and(a, b)

    barrier = pltpu.get_barrier_semaphore()

    def greet(**where):
        pl.semaphore_signal(barrier, inc=1, device_id=where, device_id_type=MESH)

    greet(fsdp=sibling)
    for k in range(1, nt_):
        greet(tensor=lax.rem(t + k, nt_))
    pl.when(y > 0)(lambda: greet(fsdp=f - 2))
    pl.when(y < ny - 1)(lambda: greet(fsdp=f + 2))
    pl.when(s > 0)(lambda: greet(section=s - 1, fsdp=partner))
    pl.when(also(s > 0, between))(lambda: greet(section=s - 1))
    links = jnp.where(between, 2, 1)
    partners = nt_ + jnp.where(y > 0, 1, 0) + jnp.where(y < ny - 1, 1, 0)
    partners = partners + links * jnp.where(s < ns - 1, 1, 0)
    pl.semaphore_wait(barrier, partners)

    def answer(**where):
        pl.semaphore_signal(open_sem, inc=1, device_id=where, device_id_type=MESH)

    pl.when(s < ns - 1)(lambda: answer(section=s + 1, fsdp=partner))
    pl.when(also(s < ns - 1, between))(lambda: answer(section=s + 1))

    def home(block, n):
        here, there = (wq, WQ) if n < PARTS else (wo, WO)
        at = (n % PARTS) * piece
        row = pl.multiple_of((2 * block + core) * depth + at, 16)
        return here.at[0, pl.ds(at, piece)], there.at[pl.ds(row, piece)]

    def far(block, n):
        there = WQ if n < PARTS else WO
        row = pl.multiple_of((2 * block + 1 - core) * depth + (n % PARTS) * piece, 16)
        return there.at[pl.ds(row, piece)]

    def own_sends(n):
        here, there = home(y, n)
        up = remote(here, there, own_sem.at[0, n], line_recv.at[0, 0, n], fsdp=jnp.minimum(f + 2, 2 * ny - 1))
        down = remote(here, there, own_sem.at[1, n], line_recv.at[1, 0, n], fsdp=jnp.maximum(f - 2, 0))
        over = remote(here, there, own_sem.at[2, n], sib_recv.at[0, ny - 1, n], fsdp=sibling)
        return up, down, over

    def start_own(n):
        up, down, over = own_sends(n)
        pl.when(y < ny - 1)(lambda: up.start())
        pl.when(y > 0)(lambda: down.start())
        over.start()

    def finish_own(n):
        up, down, over = own_sends(n)
        pl.when(y < ny - 1)(lambda: up.wait_send())
        pl.when(y > 0)(lambda: down.wait_send())
        over.wait_send()

    def line(d, j, n):
        block = y - 1 - j if d == 0 else y + 1 + j
        valid = block >= 0 if d == 0 else block <= ny - 1
        goes_on = jnp.logical_and(valid, y < ny - 1 if d == 0 else y > 0)
        block = jnp.clip(block, 0, ny - 1)
        there = home(block, n)[1]
        onward = jnp.clip(f + (2 if d == 0 else -2), 0, 2 * ny - 1)
        nxt = None
        if j < ny - 2:
            nxt = remote(there, there, line_send.at[d, j, n], line_recv.at[d, j + 1, n], fsdp=onward)
        got = remote(there, there, line_send.at[d, j, n], line_recv.at[d, j, n], fsdp=sibling)
        over = remote(there, there, sib_send.at[d, j, n], sib_recv.at[d, j, n], fsdp=sibling)
        other = far(block, n)
        sib = remote(other, other, sib_send.at[d, j, n], sib_recv.at[d, j, n], fsdp=sibling)
        return valid, goes_on, got, nxt, over, sib

    def pass_on(j, n):
        for d in range(2):
            _, goes_on, _, nxt, _, _ = line(d, j, n)
            pl.when(goes_on)(lambda: nxt.start())

    def relay(j, n, hold=False):
        for d in range(2):
            valid, goes_on, got, nxt, over, _ = line(d, j, n)

            @pl.when(valid)
            def _():
                got.wait_recv()

            if nxt is not None and not hold:
                pl.when(goes_on)(lambda: nxt.start())
            pl.when(valid)(lambda: over.start())

    def finish_line(j, n):
        for d in range(2):
            valid, goes_on, _, nxt, over, _ = line(d, j, n)
            if nxt is not None:
                pl.when(goes_on)(lambda: nxt.wait_send())
            pl.when(valid)(lambda: over.wait_send())

    def own_from_sibling(n):
        other = far(y, n)
        remote(other, other, own_sem.at[2, n], sib_recv.at[0, ny - 1, n], fsdp=sibling).wait_recv()

    def from_sibling(j, n):
        for d in range(2):
            valid, _, _, _, _, sib = line(d, j, n)
            pl.when(valid)(lambda: sib.wait_recv())

    for n in range(PARTS):
        start_own(n)

    own_q = pltpu.make_async_copy(wq.at[0], WQ.at[pl.ds(pl.multiple_of(f * depth, 16), depth)], loc_sem.at[0])
    own_o = pltpu.make_async_copy(wo.at[0], WO.at[pl.ds(pl.multiple_of(f * depth, 16), depth)], loc_sem.at[1])
    saved = pltpu.make_async_copy(stash.at[0], ST, loc_sem.at[2])
    saved.start()

    def hop1(i, g):
        src = (sent, returned)[i].at[0, mine]
        place = (above, below)[i]
        to = partner if g else f
        return remote(src, HOP1.at[i, g], hop1_send.at[i], hop1_recv.at[i, g], section=place, fsdp=to)

    goes = (s < ns - 1, s > 0)
    comes = (s > 0, s < ns - 1)
    edge = (first, last)
    first_in = (X1, G1)
    second_in = (X2, G2)
    at_hand = (fresh, loss)

    def send_hop1(i):
        pl.when(also(goes[i], between))(lambda: hop1(i, 0).start())
        pl.when(also(goes[i], end))(lambda: hop1(i, 1).start())

    own_in = [pltpu.make_async_copy(at_hand[i].at[0, mine], HOP1.at[i, 0], hop1_recv.at[i, 0]) for i in range(2)]
    own_in2 = [pltpu.make_async_copy(at_hand[i].at[1], second_in[i], loc_sem.at[5 + i]) for i in range(2)]
    guest_in = [
        remote(at_hand[i].at[0, mine], HOP1.at[i, 1], guest_send.at[i], hop1_recv.at[i, 1], fsdp=partner) for i in range(2)
    ]
    guest_stash = remote(S1.at[0], S1.at[1], guest_send.at[2], guest_recv.at[0], fsdp=partner)
    guest_frames = remote(frames, FG, guest_send.at[3], guest_recv.at[1], fsdp=partner)
    send_hop1(0)
    for i in range(2):
        pl.when(also(edge[i], between))(lambda: own_in[i].start())
        pl.when(also(edge[i], end))(lambda: guest_in[i].start())
        pl.when(edge[i])(lambda: own_in2[i].start())
    pl.when(end)(lambda: guest_frames.start())
    own_q.start()
    own_o.start()

    far_first = sorted(range(1, nt_), key=lambda k: -min(k, nt_ - k))

    def peer(k):
        return lax.rem(t + k, nt_)

    def part_of(k):
        return pl.ds(pl.multiple_of(lax.rem(t + k, nt_) * cut, cut), cut)

    def spread1(i):
        return [
            remote(HOP1.at[i], first_in[i].at[:, mine], ag_send.at[i, k - 1, 0], ag_recv.at[i, k - 1, 0], tensor=peer(k))
            for k in far_first
        ]

    def spread1_in(i):
        copies = []
        for k in far_first:
            there = first_in[i].at[:, part_of(nt_ - k)]
            copies.append(remote(there, there, ag_send.at[i, k - 1, 0], ag_recv.at[i, k - 1, 0], tensor=peer(k)))
        return copies

    def spread(i, src, dst, b):
        at = cols(b)
        return [
            remote(src.at[:, at], dst.at[mine, at], ag_send.at[i, k - 1, b], ag_recv.at[i, k - 1, b], tensor=peer(k))
            for k in far_first
        ]

    def spread_in(i, dst, b):
        copies = []
        for k in far_first:
            there = dst.at[part_of(nt_ - k), cols(b)]
            copies.append(remote(there, there, ag_send.at[i, k - 1, b], ag_recv.at[i, k - 1, b], tensor=peer(k)))
        return copies

    def hop2(i, g, b):
        place = (above, below)[i]
        to = partner if g else f
        return remote(
            SL1.at[i, g, :, cols(b)], HOP2.at[i, :, cols(b)], hop2_send.at[i, g, b], hop2_recv.at[i, b], section=place, fsdp=to
        )

    def gather2(i, b):
        hop2(i, 0, b).wait_recv()
        for c in spread(2 + i, HOP2.at[i], second_in[i], b):
            c.start()
        second_in[i][mine, cols(b)] = HOP2[i, :, cols(b)]

    def gathered2(i, b):
        for c in spread_in(2 + i, second_in[i], b):
            c.wait_recv()

    def norm(x):
        xf = x.astype(F32)
        r = lax.rsqrt(jnp.mean(xf * xf, -1, keepdims=True) + 1e-05)
        return (xf * r).astype(BF), r

    def allowed(fr):
        fr = jnp.broadcast_to(fr, (rows, rows))
        ok = jnp.where(fr <= fr.T, 1.0, 0.0)
        return jnp.concatenate([ok] * group, axis=0) > 0.5

    def chosen(tick, a, b):
        w = plan[0, tick].astype(F32)
        return a.astype(F32) * (1.0 - w) + b.astype(F32) * w

    def project(m0, m1):
        def block(i, carry):
            at = pl.ds(pl.multiple_of(i * WIDE, 128), WIDE)
            MX[m0:m1, at] = nn(XN[m0:m1, :], WQ[:, at]).astype(BF)
            return carry

        lax.fori_loop(0, WQ.shape[1] // WIDE, block, 0)

    fw, b1, b2 = (0, rows), (2 * rows, 3 * rows), 4 * rows

    def heads(m0, first_head):
        return jnp.concatenate(
            [MX[m0 : m0 + rows, (first_head + g) * HS : (first_head + g + 1) * HS] for g in range(group)], axis=0
        )

    def probs(m0, k, ok):
        key = MX[m0 : m0 + rows, (qh + k) * HS : (qh + k + 1) * HS]
        w = jnp.where(ok, jnp.exp(nt(heads(m0, k * group), key) * scale), 0.0)
        return w / jnp.sum(w, -1, keepdims=True)

    def attend(m0, ok):
        for k in range(kh):
            p = probs(m0, k, ok).astype(BF)
            ctx = nn(p, MX[m0 : m0 + rows, (qh + kh + k) * HS : (qh + kh + k + 1) * HS]).astype(BF)
            for g in range(group):
                CT[m0 : m0 + rows, (k * group + g) * HS : (k * group + g + 1) * HS] = ctx[g * rows : (g + 1) * rows]

    def keep_probs(slot, m0, ok):
        for k in range(kh):
            PR[slot, k] = probs(m0, k, ok)

    def send1(i, b):
        return [
            remote(
                PP1.at[i, :, part_of(k), cols(b)], RB1.at[i, k - 1, :, :, cols(b)],
                rs_send.at[i, k - 1, b], rs_recv.at[i, k - 1, b], tensor=peer(k),
            )
            for k in far_first
        ]

    def send2(i, b):
        return [
            remote(
                PP2.at[i, part_of(k), cols(b)], RB2.at[i, k - 1, :, cols(b)],
                rs_send.at[2 + i, k - 1, b], rs_recv.at[2 + i, k - 1, b], tensor=peer(k),
            )
            for k in far_first
        ]

    def reduced1(i, b):
        for c in send1(i, b):
            c.wait_recv()
        for g in range(2):
            total = PP1[i, g, mine, cols(b)].astype(F32)
            for k in range(1, nt_):
                total = total + RB1[i, k - 1, g, :, cols(b)].astype(F32)
            SL1[i, g, :, cols(b)] = (first_in[i][g, mine, cols(b)].astype(F32) + total).astype(BF)
        for g in (1, 0):
            pl.when(goes[i])(lambda: hop2(i, g, b).start())

    def reduced2(i, b):
        for c in send2(i, b):
            c.wait_recv()
        total = PP2[i, mine, cols(b)].astype(F32)
        for k in range(1, nt_):
            total = total + RB2[i, k - 1, :, cols(b)].astype(F32)
        SL2[i, :, cols(b)] = (second_in[i][mine, cols(b)].astype(F32) + total).astype(BF)
        for c in spread(4 + i, SL2.at[i], (out_f, out_b)[i].at[0], b):
            c.start()

    def heads_back(slot, m0, d0, dc):
        for k in range(kh):
            value = MX[m0 : m0 + rows, (qh + kh + k) * HS : (qh + kh + k + 1) * HS]
            key = MX[m0 : m0 + rows, (qh + k) * HS : (qh + k + 1) * HS]
            q = heads(m0, k * group)
            dctx = jnp.concatenate(
                [dc[:, (k * group + g) * HS : (k * group + g + 1) * HS] for g in range(group)], axis=0
            )
            p = PR[slot, k]
            dp = nt(dctx, value).astype(BF).astype(F32)
            ds = (p * (dp - jnp.sum(dp * p, -1, keepdims=True)) * scale).astype(BF)
            dq = nn(ds, key).astype(BF)
            dk = tn(ds, q).astype(BF)
            dv = tn(p.astype(BF), dctx).astype(BF)
            for g in range(group):
                DM[d0 : d0 + rows, (k * group + g) * HS : (k * group + g + 1) * HS] = dq[g * rows : (g + 1) * rows]
            DM[d0 : d0 + rows, (qh + k) * HS : (qh + k + 1) * HS] = dk
            DM[d0 : d0 + rows, (qh + kh + k) * HS : (qh + kh + k + 1) * HS] = dv
        return (
            jnp.sum(DM[d0 : d0 + rows, :].astype(F32) * MX[m0 : m0 + rows, :].astype(F32), -1, keepdims=True) / width
        )

    def norm_back(slot, dn, x, mean):
        r = RN[slot][:, 0:1]
        return (r * (dn.astype(BF).astype(F32) - x.astype(F32) * r * mean)).astype(BF)

    def turn(b, carry):
        for c in range(0, wide, HS):
            at = pl.ds(pl.multiple_of(b * wide + c, HS), HS)
            WT[:, at] = WQ[at, :].T
        return carry

    def turn_all():
        lax.fori_loop(0, ny, turn, 0)

    in_pieces = range(PARTS)
    out_pieces = range(PARTS, 2 * PARTS)

    def prepare(slot, m0, x):
        xn, r = norm(x)
        XN[m0 : m0 + rows, :] = xn
        RN[slot] = jnp.broadcast_to(r, (rows, HS))

    saved.wait()
    S1[0] = chosen(0, ST[0], ST[1]).astype(BF)
    pl.when(end)(lambda: guest_stash.start())
    x = chosen(1, ST[0], ST[1]).astype(BF)
    S2[...] = x
    prepare(2, b2, x)
    for n in in_pieces:
        relay(0, n)
    for n in out_pieces:
        start_own(n)

    pl.when(s > 0)(lambda: pl.semaphore_wait(open_sem, links))
    send_hop1(1)

    def arrive1(i):
        for g in range(2):
            hop1(i, g).wait_recv()
        for c in spread1(i):
            c.start()
        for g in range(2):
            first_in[i][g, mine, :] = HOP1[i, g]

    @pl.when(between)
    def _():
        arrive1(0)
        prepare(0, b1[0], S1[0])

    for n in in_pieces:
        relay(1, n)
        if n == 0:
            pl.when(between)(lambda: arrive1(1))

    @pl.when(between)
    def _():
        for n in out_pieces:
            relay(0, n)

    for j in range(2, ny - 1):
        for n in in_pieces:
            relay(j, n)

    @pl.when(between)
    def _():
        for i in range(2):
            for c in spread1_in(i):
                c.wait_recv()

        guest_stash.wait_recv()
        guest_frames.wait_recv()
        prepare(1, b1[1], S1[1])
        for g in range(2):
            XN[fw[g] : fw[g] + rows, :] = norm(X1[g])[0]

    own_q.wait()
    for n in in_pieces:
        own_from_sibling(n)
        for j in range(ny - 1):
            from_sibling(j, n)
    fr = frames[...].astype(F32)

    def keep_second():
        keep_probs(2, b2, allowed(chosen(1, fr[0:1], fr[1:2])))

    def arrive(i):
        for b in range(ny):
            pl.when(comes[i])(lambda: gather2(i, b))

    def second_forward():
        pl.when(edge[0])(lambda: own_in2[0].wait())
        squares = jnp.zeros((rows, 1), F32)
        mixed = jnp.zeros((rows, WQ.shape[1]), F32)
        for b in range(ny):
            pl.when(comes[0])(lambda: gathered2(0, b))
            x = X2[:, cols(b)]
            mixed = mixed + nn(x, WQ[cols(b), :])
            squares = squares + jnp.sum(x.astype(F32) * x.astype(F32), -1, keepdims=True)
        MX[0:rows, :] = (mixed * lax.rsqrt(squares / width + 1e-05)).astype(BF)
        attend(0, allowed(fr[1:2]))

    def block(i):
        return jnp.where(y < ny // 2, i, ny - 1 - i)

    def second_output(i):
        b = block(i)
        PP2[0, :, cols(b)] = nt(CT[0:rows, :], WO[cols(b), :]).astype(BF)
        for c in send2(0, b):
            c.start()

    def second_grad(i):
        b = block(i)
        if i == 0:
            pl.when(edge[1])(lambda: own_in2[1].wait())
        pl.when(comes[1])(lambda: gathered2(1, b))
        part = nn(G2[:, cols(b)], WO[cols(b), :])
        DA[0:rows, :] = part if i == 0 else DA[0:rows, :] + part

    @pl.when(end)
    def _():
        project(b2, b2 + rows)
        keep_second()
        turn_all()
        own_o.wait()
        for n in out_pieces:
            own_from_sibling(n)
        for j in range(ny - 2):
            for n in out_pieces:
                relay(j, n)
            for n in out_pieces:
                from_sibling(j, n)
        pl.when(jnp.logical_not(wrap))(lambda: arrive(0))
        for n in out_pieces:
            relay(ny - 2, n)
        arrive(1)
        pl.when(jnp.logical_not(wrap))(second_forward)
        for n in out_pieces:
            from_sibling(ny - 2, n)

        @pl.when(jnp.logical_not(wrap))
        def _():
            for i in range(ny):
                second_output(i)

        for i in range(ny):
            second_grad(i)

    @pl.when(between)
    def _():
        project(0, b2 + rows)
        guest = FG[...].astype(F32)
        marks = (fr, guest)
        for g in range(2):
            attend(fw[g], allowed(marks[g][0:1]))
        for g in range(2):
            keep_probs(g, b1[g], allowed(chosen(0, marks[g][0:1], marks[g][1:2])))
        turn_all()
        order = (1, 0, 2, 3)
        for i in range(ny):
            if i == 0:
                own_o.wait()
                for n in out_pieces:
                    own_from_sibling(n)
            elif i == 1:
                for n in out_pieces:
                    from_sibling(0, n)
            elif i == 3:
                for j in range(1, ny - 1):
                    for n in out_pieces:
                        relay(j, n, hold=n == out_pieces[-1])
                    for n in out_pieces:
                        from_sibling(j, n)
            b = jnp.where(y < ny // 2, order[i], ny - 1 - order[i])
            weight = WO[cols(b), :]
            part = nt(CT[...], weight).astype(BF)
            for g in range(2):
                PP1[0, g, :, cols(b)] = part[g * rows : (g + 1) * rows]
            for c in send1(0, b):
                c.start()
            grad = jnp.concatenate([G1[0, :, cols(b)], G1[1, :, cols(b)]], axis=0)
            part = nn(grad, weight)
            DA[...] = part if i == 0 else DA[...] + part
        mean = [heads_back(g, b1[g], g * rows, DA[g * rows : (g + 1) * rows, :].astype(BF)) for g in range(2)]
        for b in range(ny):
            dn = nn(DM[...], WT[:, cols(b)])
            for g in range(2):
                PP1[1, g, :, cols(b)] = norm_back(g, dn[g * rows : (g + 1) * rows], S1[g, :, cols(b)], mean[g])
            for c in send1(1, b):
                c.start()
        for b in range(ny):
            reduced1(0, b)
        for j in range(1, ny - 2):
            pass_on(j, out_pieces[-1])
        for b in range(ny):
            reduced1(1, b)
        pl.when(jnp.logical_not(wrap))(lambda: arrive(0))
        keep_second()
        arrive(1)

        @pl.when(jnp.logical_not(wrap))
        def _():
            second_forward()
            for i in range(ny):
                second_output(i)

        for i in range(ny):
            second_grad(i)

    def second_heads():
        return heads_back(2, b2, 0, DA[0:rows, :].astype(BF))

    def second_input(mean, b):
        PP2[1, :, cols(b)] = norm_back(2, nn(DM[0:rows, :], WT[:, cols(b)]), S2[:, cols(b)], mean)
        for c in send2(1, b):
            c.start()

    @pl.when(jnp.logical_not(wrap))
    def _():
        mean = second_heads()
        for b in range(ny):
            second_input(mean, b)
        for i in range(2):
            for j in range(ny):
                reduced2(i, block(j) if i == 0 else j)

    @pl.when(wrap)
    def _():
        arrive(0)
        mean = second_heads()
        for b in range(ny):
            second_input(mean, b)
        second_forward()
        for i in range(ny):
            second_output(i)
        for i in (1, 0):
            for b in range(ny):
                reduced2(i, b)

    keep_f = pltpu.make_async_copy(SL2.at[0], out_f.at[0, mine], loc_sem.at[7])
    keep_b = pltpu.make_async_copy(SL2.at[1], out_b.at[0, mine], loc_sem.at[8])
    keep_f.start()
    keep_b.start()

    for n in range(2 * PARTS):
        finish_own(n)
        for j in range(ny - 1):
            finish_line(j, n)

    @pl.when(end)
    def _():
        guest_stash.wait_send()
        guest_frames.wait_send()

    for i in range(2):
        pl.when(goes[i])(lambda: hop1(i, 0).wait_send())
        pl.when(also(edge[i], end))(lambda: guest_in[i].wait_send())

        @pl.when(between)
        def _():
            for c in spread1(i):
                c.wait_send()

            for b in range(ny):
                for c in send1(i, b):
                    c.wait_send()
                for g in range(2):
                    pl.when(goes[i])(lambda: hop2(i, g, b).wait_send())

        for b in range(ny):
            for c in send2(i, b):
                c.wait_send()

            @pl.when(comes[i])
            def _():
                for c in spread(2 + i, HOP2.at[i], second_in[i], b):
                    c.wait_send()

    for i, out in ((0, out_f), (1, out_b)):
        for b in range(ny):
            for c in spread_in(4 + i, out.at[0], b):
                c.wait_recv()
            for c in spread(4 + i, SL2.at[i], out.at[0], b):
                c.wait_send()
    keep_f.wait()
    keep_b.wait()


def body(fresh, sent, stash, returned, loss_grads, plan, frame_ids, qkv_weight, out_weight):
    nt_ = lax.axis_size("tensor")
    n_fsdp = lax.axis_size("fsdp")
    ny = n_fsdp // 2
    _, rows, width = sent.shape
    depth, columns = qkv_weight.shape[1:]
    inner = out_weight.shape[2]
    kh = (columns - inner) // (2 * HS)
    group = inner // HS // kh
    cut = rows // nt_
    dma = pltpu.SemaphoreType.DMA
    anywhere = pl.BlockSpec(memory_space=pl.ANY)
    whole = pl.BlockSpec(memory_space=pltpu.VMEM)
    act = pltpu.VMEM((rows, width), BF)
    acts = pltpu.VMEM((2, rows, width), BF)
    return pl.pallas_call(
        kernel,
        out_shape=[jax.ShapeDtypeStruct(sent.shape, BF)] * 2,
        in_specs=[anywhere] * 5 + [pl.BlockSpec(memory_space=pltpu.SMEM), whole] + [anywhere] * 2,
        out_specs=[anywhere] * 2,
        scratch_shapes=[
            pltpu.VMEM((n_fsdp * depth, columns), BF),
            pltpu.VMEM((n_fsdp * depth, inner), BF),
            pltpu.VMEM((columns, n_fsdp * depth), BF),
            acts, acts, acts, act, act, act, acts,
            pltpu.VMEM(frame_ids.shape, jnp.int32),
            pltpu.VMEM((5 * rows, width), BF),
            pltpu.VMEM((3, rows, HS), F32),
            pltpu.VMEM((5 * rows, columns), BF),
            pltpu.VMEM((3, kh, group * rows, rows), F32),
            pltpu.VMEM((2 * rows, inner), BF),
            pltpu.VMEM((2 * rows, columns), BF),
            pltpu.VMEM((2 * rows, inner), F32),
            pltpu.VMEM((2, 2, rows, width), BF),
            pltpu.VMEM((2, nt_ - 1, 2, cut, width), BF),
            pltpu.VMEM((2, 2, cut, width), BF),
            pltpu.VMEM((2, 2, cut, width), BF),
            pltpu.VMEM((2, rows, width), BF),
            pltpu.VMEM((2, nt_ - 1, cut, width), BF),
            pltpu.VMEM((2, cut, width), BF),
            pltpu.VMEM((2, cut, width), BF),
            dma((3, 2 * PARTS)),
            dma((2, ny - 1, 2 * PARTS)),
            dma((2, ny - 1, 2 * PARTS)),
            dma((2, ny - 1, 2 * PARTS)),
            dma((2, ny, 2 * PARTS)),
            dma((9,)),
            dma((4,)),
            dma((2,)),
            dma((2,)),
            dma((2, 2)),
            dma((2, 2, ny)),
            dma((2, ny)),
            dma((6, nt_ - 1, ny)),
            dma((6, nt_ - 1, ny)),
            dma((4, nt_ - 1, ny)),
            dma((4, nt_ - 1, ny)),
            pltpu.SemaphoreType.REGULAR,
        ],
        compiler_params=pltpu.CompilerParams(
            collective_id=0, has_side_effects=True, vmem_limit_bytes=60 << 20
        ),
        name="relay",
    )(fresh, sent, stash, returned, loss_grads, plan, frame_ids, qkv_weight, out_weight)


def solution(mesh):
    placed = (
        P(None, "fsdp", None),
        P("section", "fsdp", None),
        P("section", None, "fsdp", None),
        P("section", "fsdp", None),
        P(None, "fsdp", None),
        P("section", None),
        P(None, "fsdp"),
        P("section", "fsdp", "tensor"),
        P("section", "fsdp", "tensor"),
    )
    return jax.shard_map(
        body,
        mesh=mesh,
        in_specs=placed,
        out_specs=(P("section", "fsdp", None), P("section", "fsdp", None)),
        check_vma=False,
    )
```

```python
import jax
import jax.numpy as jnp
from jax import lax
from jax.experimental import pallas as pl
from jax.experimental.pallas import tpu as pltpu
from jax.sharding import PartitionSpec as P

HS = 128
MESH = pl.DeviceIdType.MESH
BF = jnp.bfloat16
F32 = jnp.float32
PARTS = 2
WIDE = 512


def nn(a, b):
    return jnp.dot(a, b, preferred_element_type=F32)


def nt(a, b):
    return lax.dot_general(a, b, (((1,), (1,)), ((), ())), preferred_element_type=F32)


def tn(a, b):
    return lax.dot_general(a, b, (((0,), (0,)), ((), ())), preferred_element_type=F32)


def kernel(
    fresh, sent, stash, returned, loss, plan, frames, wq, wo, out_f, out_b,
    WQ, WO, WT, X1, G1, S1, X2, G2, S2, ST, FG, XN, RN, MX, PR, CT, DM, DA, PP1, RB1, SL1, HOP1, PP2, RB2, SL2, HOP2,
    own_sem, line_send, line_recv, sib_send, sib_recv, loc_sem, guest_send, guest_recv, hop1_send, hop1_recv,
    hop2_send, hop2_recv, ag_send, ag_recv, rs_send, rs_recv, open_sem,
):
    s = lax.axis_index("section")
    f = lax.axis_index("fsdp")
    t = lax.axis_index("tensor")
    ns, nt_ = lax.axis_size("section"), lax.axis_size("tensor")
    ny = lax.axis_size("fsdp") // 2
    y, core = f // 2, lax.rem(f, 2)
    sibling = 2 * y + 1 - core
    rows, width = X2.shape
    cut = rows // nt_
    depth = wq.shape[1]
    piece = depth // PARTS
    qh = WO.shape[1] // HS
    kh = (WQ.shape[1] // HS - qh) // 2
    group = qh // kh
    scale = HS**-0.5
    first, last = s == 0, s == ns - 1
    mine = pl.ds(pl.multiple_of(t * cut, cut), cut)
    wide = width // ny
    between = jnp.logical_and(y > 0, y < ny - 1)
    end = jnp.logical_not(between)
    partner = jnp.where(jnp.logical_xor(y < ny // 2, between), f + 2, f - 2)
    above, below = jnp.minimum(s + 1, ns - 1), jnp.maximum(s - 1, 0)

    def cols(b):
        return pl.ds(pl.multiple_of(b * wide, 128), wide)

    def remote(src, dst, ss, rs, **where):
        return pltpu.make_async_remote_copy(
            src_ref=src, dst_ref=dst, send_sem=ss, recv_sem=rs, device_id=where, device_id_type=MESH
        )

    def also(a, b):
        return jnp.logical_and(a, b)

    barrier = pltpu.get_barrier_semaphore()

    def greet(**where):
        pl.semaphore_signal(barrier, inc=1, device_id=where, device_id_type=MESH)

    greet(fsdp=sibling)
    for k in range(1, nt_):
        greet(tensor=lax.rem(t + k, nt_))
    pl.when(y > 0)(lambda: greet(fsdp=f - 2))
    pl.when(y < ny - 1)(lambda: greet(fsdp=f + 2))
    pl.when(s > 0)(lambda: greet(section=s - 1, fsdp=partner))
    pl.when(also(s > 0, between))(lambda: greet(section=s - 1))
    links = jnp.where(between, 2, 1)
    partners = nt_ + jnp.where(y > 0, 1, 0) + jnp.where(y < ny - 1, 1, 0)
    partners = partners + links * jnp.where(s < ns - 1, 1, 0)
    pl.semaphore_wait(barrier, partners)

    def answer(**where):
        pl.semaphore_signal(open_sem, inc=1, device_id=where, device_id_type=MESH)

    pl.when(s < ns - 1)(lambda: answer(section=s + 1, fsdp=partner))
    pl.when(also(s < ns - 1, between))(lambda: answer(section=s + 1))

    def home(block, n):
        here, there = (wq, WQ) if n < PARTS else (wo, WO)
        at = (n % PARTS) * piece
        row = pl.multiple_of((2 * block + core) * depth + at, 16)
        return here.at[0, pl.ds(at, piece)], there.at[pl.ds(row, piece)]

    def far(block, n):
        there = WQ if n < PARTS else WO
        row = pl.multiple_of((2 * block + 1 - core) * depth + (n % PARTS) * piece, 16)
        return there.at[pl.ds(row, piece)]

    def own_sends(n):
        here, there = home(y, n)
        up = remote(here, there, own_sem.at[0, n], line_recv.at[0, 0, n], fsdp=jnp.minimum(f + 2, 2 * ny - 1))
        down = remote(here, there, own_sem.at[1, n], line_recv.at[1, 0, n], fsdp=jnp.maximum(f - 2, 0))
        over = remote(here, there, own_sem.at[2, n], sib_recv.at[0, ny - 1, n], fsdp=sibling)
        return up, down, over

    def start_own(n):
        up, down, over = own_sends(n)
        pl.when(y < ny - 1)(lambda: up.start())
        pl.when(y > 0)(lambda: down.start())
        over.start()

    def finish_own(n):
        up, down, over = own_sends(n)
        pl.when(y < ny - 1)(lambda: up.wait_send())
        pl.when(y > 0)(lambda: down.wait_send())
        over.wait_send()

    def line(d, j, n):
        block = y - 1 - j if d == 0 else y + 1 + j
        valid = block >= 0 if d == 0 else block <= ny - 1
        goes_on = jnp.logical_and(valid, y < ny - 1 if d == 0 else y > 0)
        block = jnp.clip(block, 0, ny - 1)
        there = home(block, n)[1]
        onward = jnp.clip(f + (2 if d == 0 else -2), 0, 2 * ny - 1)
        nxt = None
        if j < ny - 2:
            nxt = remote(there, there, line_send.at[d, j, n], line_recv.at[d, j + 1, n], fsdp=onward)
        got = remote(there, there, line_send.at[d, j, n], line_recv.at[d, j, n], fsdp=sibling)
        over = remote(there, there, sib_send.at[d, j, n], sib_recv.at[d, j, n], fsdp=sibling)
        other = far(block, n)
        sib = remote(other, other, sib_send.at[d, j, n], sib_recv.at[d, j, n], fsdp=sibling)
        return valid, goes_on, got, nxt, over, sib

    def pass_on(j, n):
        for d in range(2):
            _, goes_on, _, nxt, _, _ = line(d, j, n)
            pl.when(goes_on)(lambda: nxt.start())

    def relay(j, n, hold=False):
        for d in range(2):
            valid, goes_on, got, nxt, over, _ = line(d, j, n)

            @pl.when(valid)
            def _():
                got.wait_recv()

            if nxt is not None and not hold:
                pl.when(goes_on)(lambda: nxt.start())
            pl.when(valid)(lambda: over.start())

    def finish_line(j, n):
        for d in range(2):
            valid, goes_on, _, nxt, over, _ = line(d, j, n)
            if nxt is not None:
                pl.when(goes_on)(lambda: nxt.wait_send())
            pl.when(valid)(lambda: over.wait_send())

    def own_from_sibling(n):
        other = far(y, n)
        remote(other, other, own_sem.at[2, n], sib_recv.at[0, ny - 1, n], fsdp=sibling).wait_recv()

    def from_sibling(j, n):
        for d in range(2):
            valid, _, _, _, _, sib = line(d, j, n)
            pl.when(valid)(lambda: sib.wait_recv())

    for n in range(PARTS):
        start_own(n)

    own_q = pltpu.make_async_copy(wq.at[0], WQ.at[pl.ds(pl.multiple_of(f * depth, 16), depth)], loc_sem.at[0])
    own_o = pltpu.make_async_copy(wo.at[0], WO.at[pl.ds(pl.multiple_of(f * depth, 16), depth)], loc_sem.at[1])
    saved = pltpu.make_async_copy(stash.at[0], ST, loc_sem.at[2])
    saved.start()

    def hop1(i, g):
        src = (sent, returned)[i].at[0, mine]
        place = (above, below)[i]
        to = partner if g else f
        return remote(src, HOP1.at[i, g], hop1_send.at[i], hop1_recv.at[i, g], section=place, fsdp=to)

    goes = (s < ns - 1, s > 0)
    comes = (s > 0, s < ns - 1)
    edge = (first, last)
    first_in = (X1, G1)
    second_in = (X2, G2)
    at_hand = (fresh, loss)

    def send_hop1(i):
        pl.when(also(goes[i], between))(lambda: hop1(i, 0).start())
        pl.when(also(goes[i], end))(lambda: hop1(i, 1).start())

    own_in = [pltpu.make_async_copy(at_hand[i].at[0, mine], HOP1.at[i, 0], hop1_recv.at[i, 0]) for i in range(2)]
    own_in2 = [pltpu.make_async_copy(at_hand[i].at[1], second_in[i], loc_sem.at[5 + i]) for i in range(2)]
    guest_in = [
        remote(at_hand[i].at[0, mine], HOP1.at[i, 1], guest_send.at[i], hop1_recv.at[i, 1], fsdp=partner) for i in range(2)
    ]
    guest_stash = remote(S1.at[0], S1.at[1], guest_send.at[2], guest_recv.at[0], fsdp=partner)
    guest_frames = remote(frames, FG, guest_send.at[3], guest_recv.at[1], fsdp=partner)
    send_hop1(0)
    for i in range(2):
        pl.when(also(edge[i], between))(lambda: own_in[i].start())
        pl.when(also(edge[i], end))(lambda: guest_in[i].start())
        pl.when(edge[i])(lambda: own_in2[i].start())
    pl.when(end)(lambda: guest_frames.start())
    own_q.start()
    own_o.start()

    far_first = sorted(range(1, nt_), key=lambda k: -min(k, nt_ - k))

    def peer(k):
        return lax.rem(t + k, nt_)

    def part_of(k):
        return pl.ds(pl.multiple_of(lax.rem(t + k, nt_) * cut, cut), cut)

    def spread1(i):
        return [
            remote(HOP1.at[i], first_in[i].at[:, mine], ag_send.at[i, k - 1, 0], ag_recv.at[i, k - 1, 0], tensor=peer(k))
            for k in far_first
        ]

    def spread1_in(i):
        copies = []
        for k in far_first:
            there = first_in[i].at[:, part_of(nt_ - k)]
            copies.append(remote(there, there, ag_send.at[i, k - 1, 0], ag_recv.at[i, k - 1, 0], tensor=peer(k)))
        return copies

    def spread(i, src, dst, b):
        at = cols(b)
        return [
            remote(src.at[:, at], dst.at[mine, at], ag_send.at[i, k - 1, b], ag_recv.at[i, k - 1, b], tensor=peer(k))
            for k in far_first
        ]

    def spread_in(i, dst, b):
        copies = []
        for k in far_first:
            there = dst.at[part_of(nt_ - k), cols(b)]
            copies.append(remote(there, there, ag_send.at[i, k - 1, b], ag_recv.at[i, k - 1, b], tensor=peer(k)))
        return copies

    def hop2(i, g, b):
        place = (above, below)[i]
        to = partner if g else f
        return remote(
            SL1.at[i, g, :, cols(b)], HOP2.at[i, :, cols(b)], hop2_send.at[i, g, b], hop2_recv.at[i, b], section=place, fsdp=to
        )

    def gather2(i, b):
        hop2(i, 0, b).wait_recv()
        for c in spread(2 + i, HOP2.at[i], second_in[i], b):
            c.start()
        second_in[i][mine, cols(b)] = HOP2[i, :, cols(b)]

    def gathered2(i, b):
        for c in spread_in(2 + i, second_in[i], b):
            c.wait_recv()

    def norm(x):
        xf = x.astype(F32)
        r = lax.rsqrt(jnp.mean(xf * xf, -1, keepdims=True) + 1e-05)
        return (xf * r).astype(BF), r

    def allowed(fr):
        fr = jnp.broadcast_to(fr, (rows, rows))
        ok = jnp.where(fr <= fr.T, 1.0, 0.0)
        return jnp.concatenate([ok] * group, axis=0) > 0.5

    def chosen(tick, a, b):
        w = plan[0, tick].astype(F32)
        return a.astype(F32) * (1.0 - w) + b.astype(F32) * w

    def project(m0, m1):
        def block(i, carry):
            at = pl.ds(pl.multiple_of(i * WIDE, 128), WIDE)
            MX[m0:m1, at] = nn(XN[m0:m1, :], WQ[:, at]).astype(BF)
            return carry

        lax.fori_loop(0, WQ.shape[1] // WIDE, block, 0)

    fw, b1, b2 = (0, rows), (2 * rows, 3 * rows), 4 * rows

    def heads(m0, first_head):
        return jnp.concatenate(
            [MX[m0 : m0 + rows, (first_head + g) * HS : (first_head + g + 1) * HS] for g in range(group)], axis=0
        )

    def probs(m0, k, ok):
        key = MX[m0 : m0 + rows, (qh + k) * HS : (qh + k + 1) * HS]
        w = jnp.where(ok, jnp.exp(nt(heads(m0, k * group), key) * scale), 0.0)
        return w / jnp.sum(w, -1, keepdims=True)

    def attend(m0, ok):
        for k in range(kh):
            p = probs(m0, k, ok).astype(BF)
            ctx = nn(p, MX[m0 : m0 + rows, (qh + kh + k) * HS : (qh + kh + k + 1) * HS]).astype(BF)
            for g in range(group):
                CT[m0 : m0 + rows, (k * group + g) * HS : (k * group + g + 1) * HS] = ctx[g * rows : (g + 1) * rows]

    def keep_probs(slot, m0, ok):
        for k in range(kh):
            PR[slot, k] = probs(m0, k, ok)

    def send1(i, b):
        return [
            remote(
                PP1.at[i, :, part_of(k), cols(b)], RB1.at[i, k - 1, :, :, cols(b)],
                rs_send.at[i, k - 1, b], rs_recv.at[i, k - 1, b], tensor=peer(k),
            )
            for k in far_first
        ]

    def send2(i, b):
        return [
            remote(
                PP2.at[i, part_of(k), cols(b)], RB2.at[i, k - 1, :, cols(b)],
                rs_send.at[2 + i, k - 1, b], rs_recv.at[2 + i, k - 1, b], tensor=peer(k),
            )
            for k in far_first
        ]

    def reduced1(i, b):
        for c in send1(i, b):
            c.wait_recv()
        for g in range(2):
            total = PP1[i, g, mine, cols(b)].astype(F32)
            for k in range(1, nt_):
                total = total + RB1[i, k - 1, g, :, cols(b)].astype(F32)
            SL1[i, g, :, cols(b)] = (first_in[i][g, mine, cols(b)].astype(F32) + total).astype(BF)
        for g in (1, 0):
            pl.when(goes[i])(lambda: hop2(i, g, b).start())

    def reduced2(i, b):
        for c in send2(i, b):
            c.wait_recv()
        total = PP2[i, mine, cols(b)].astype(F32)
        for k in range(1, nt_):
            total = total + RB2[i, k - 1, :, cols(b)].astype(F32)
        SL2[i, :, cols(b)] = (second_in[i][mine, cols(b)].astype(F32) + total).astype(BF)
        for c in spread(4 + i, SL2.at[i], (out_f, out_b)[i].at[0], b):
            c.start()

    def heads_back(slot, m0, d0, dc):
        for k in range(kh):
            value = MX[m0 : m0 + rows, (qh + kh + k) * HS : (qh + kh + k + 1) * HS]
            key = MX[m0 : m0 + rows, (qh + k) * HS : (qh + k + 1) * HS]
            q = heads(m0, k * group)
            dctx = jnp.concatenate(
                [dc[:, (k * group + g) * HS : (k * group + g + 1) * HS] for g in range(group)], axis=0
            )
            p = PR[slot, k]
            dp = nt(dctx, value).astype(BF).astype(F32)
            ds = (p * (dp - jnp.sum(dp * p, -1, keepdims=True)) * scale).astype(BF)
            dq = nn(ds, key).astype(BF)
            dk = tn(ds, q).astype(BF)
            dv = tn(p.astype(BF), dctx).astype(BF)
            for g in range(group):
                DM[d0 : d0 + rows, (k * group + g) * HS : (k * group + g + 1) * HS] = dq[g * rows : (g + 1) * rows]
            DM[d0 : d0 + rows, (qh + k) * HS : (qh + k + 1) * HS] = dk
            DM[d0 : d0 + rows, (qh + kh + k) * HS : (qh + kh + k + 1) * HS] = dv
        return (
            jnp.sum(DM[d0 : d0 + rows, :].astype(F32) * MX[m0 : m0 + rows, :].astype(F32), -1, keepdims=True) / width
        )

    def norm_back(slot, dn, x, mean):
        r = RN[slot][:, 0:1]
        return (r * (dn.astype(BF).astype(F32) - x.astype(F32) * r * mean)).astype(BF)

    def turn(b, carry):
        for c in range(0, wide, HS):
            at = pl.ds(pl.multiple_of(b * wide + c, HS), HS)
            WT[:, at] = WQ[at, :].T
        return carry

    def turn_all():
        lax.fori_loop(0, ny, turn, 0)

    in_pieces = range(PARTS)
    out_pieces = range(PARTS, 2 * PARTS)

    def prepare(slot, m0, x):
        xn, r = norm(x)
        XN[m0 : m0 + rows, :] = xn
        RN[slot] = jnp.broadcast_to(r, (rows, HS))

    saved.wait()
    S1[0] = chosen(0, ST[0], ST[1]).astype(BF)
    pl.when(end)(lambda: guest_stash.start())
    x = chosen(1, ST[0], ST[1]).astype(BF)
    S2[...] = x
    prepare(2, b2, x)
    for n in in_pieces:
        relay(0, n)
    for n in out_pieces:
        start_own(n)

    pl.when(s > 0)(lambda: pl.semaphore_wait(open_sem, links))
    send_hop1(1)

    def arrive1(i):
        for g in range(2):
            hop1(i, g).wait_recv()
        for c in spread1(i):
            c.start()
        for g in range(2):
            first_in[i][g, mine, :] = HOP1[i, g]

    @pl.when(between)
    def _():
        arrive1(0)
        prepare(0, b1[0], S1[0])

    for n in in_pieces:
        relay(1, n)
        if n == 0:
            pl.when(between)(lambda: arrive1(1))

    @pl.when(between)
    def _():
        for n in out_pieces:
            relay(0, n)

    for j in range(2, ny - 1):
        for n in in_pieces:
            relay(j, n)

    @pl.when(between)
    def _():
        for i in range(2):
            for c in spread1_in(i):
                c.wait_recv()

        guest_stash.wait_recv()
        guest_frames.wait_recv()
        prepare(1, b1[1], S1[1])
        for g in range(2):
            XN[fw[g] : fw[g] + rows, :] = norm(X1[g])[0]

    own_q.wait()
    for n in in_pieces:
        own_from_sibling(n)
        for j in range(ny - 1):
            from_sibling(j, n)
    fr = frames[...].astype(F32)

    def keep_second():
        keep_probs(2, b2, allowed(chosen(1, fr[0:1], fr[1:2])))

    def arrive(i):
        for b in range(ny):
            pl.when(comes[i])(lambda: gather2(i, b))

    def second_forward():
        pl.when(edge[0])(lambda: own_in2[0].wait())
        squares = jnp.zeros((rows, 1), F32)
        mixed = jnp.zeros((rows, WQ.shape[1]), F32)
        for b in range(ny):
            pl.when(comes[0])(lambda: gathered2(0, b))
            x = X2[:, cols(b)]
            mixed = mixed + nn(x, WQ[cols(b), :])
            squares = squares + jnp.sum(x.astype(F32) * x.astype(F32), -1, keepdims=True)
        MX[0:rows, :] = (mixed * lax.rsqrt(squares / width + 1e-05)).astype(BF)
        attend(0, allowed(fr[1:2]))

    def block(i):
        return jnp.where(y < ny // 2, i, ny - 1 - i)

    def second_output(i):
        b = block(i)
        PP2[0, :, cols(b)] = nt(CT[0:rows, :], WO[cols(b), :]).astype(BF)
        for c in send2(0, b):
            c.start()

    def second_grad(i):
        b = block(i)
        if i == 0:
            pl.when(edge[1])(lambda: own_in2[1].wait())
        pl.when(comes[1])(lambda: gathered2(1, b))
        part = nn(G2[:, cols(b)], WO[cols(b), :])
        DA[0:rows, :] = part if i == 0 else DA[0:rows, :] + part

    @pl.when(end)
    def _():
        project(b2, b2 + rows)
        keep_second()
        turn_all()
        own_o.wait()
        for n in out_pieces:
            own_from_sibling(n)
        for j in range(ny - 2):
            for n in out_pieces:
                relay(j, n)
            for n in out_pieces:
                from_sibling(j, n)
        arrive(0)
        for n in out_pieces:
            relay(ny - 2, n)
        arrive(1)
        second_forward()
        for n in out_pieces:
            from_sibling(ny - 2, n)

        for i in range(ny):
            second_output(i)

        for i in range(ny):
            second_grad(i)

    @pl.when(between)
    def _():
        project(0, b2 + rows)
        guest = FG[...].astype(F32)
        marks = (fr, guest)
        for g in range(2):
            attend(fw[g], allowed(marks[g][0:1]))
        for g in range(2):
            keep_probs(g, b1[g], allowed(chosen(0, marks[g][0:1], marks[g][1:2])))
        turn_all()
        order = (1, 0, 2, 3)
        for i in range(ny):
            if i == 0:
                own_o.wait()
                for n in out_pieces:
                    own_from_sibling(n)
            elif i == 1:
                for n in out_pieces:
                    from_sibling(0, n)
            elif i == 3:
                for j in range(1, ny - 1):
                    for n in out_pieces:
                        relay(j, n, hold=n == out_pieces[-1])
                    for n in out_pieces:
                        from_sibling(j, n)
            b = jnp.where(y < ny // 2, order[i], ny - 1 - order[i])
            weight = WO[cols(b), :]
            part = nt(CT[...], weight).astype(BF)
            for g in range(2):
                PP1[0, g, :, cols(b)] = part[g * rows : (g + 1) * rows]
            for c in send1(0, b):
                c.start()
            grad = jnp.concatenate([G1[0, :, cols(b)], G1[1, :, cols(b)]], axis=0)
            part = nn(grad, weight)
            DA[...] = part if i == 0 else DA[...] + part
        mean = [heads_back(g, b1[g], g * rows, DA[g * rows : (g + 1) * rows, :].astype(BF)) for g in range(2)]
        blocks = [jnp.where(y < ny // 2, o, ny - 1 - o) for o in order]
        last_block = blocks[3]
        for i in range(3):
            reduced1(0, blocks[i])
        for b in range(ny):
            dn = nn(DM[...], WT[:, cols(b)])
            for g in range(2):
                PP1[1, g, :, cols(b)] = norm_back(g, dn[g * rows : (g + 1) * rows], S1[g, :, cols(b)], mean[g])
            for c in send1(1, b):
                c.start()
        reduced1(0, last_block)
        for j in range(1, ny - 2):
            pass_on(j, out_pieces[-1])
        for b in range(ny):
            reduced1(1, b)
        arrive(0)
        keep_second()
        arrive(1)

        second_forward()
        for i in range(ny):
            second_output(i)

        for i in range(ny):
            second_grad(i)

    def second_heads():
        return heads_back(2, b2, 0, DA[0:rows, :].astype(BF))

    def second_input(mean, b):
        PP2[1, :, cols(b)] = norm_back(2, nn(DM[0:rows, :], WT[:, cols(b)]), S2[:, cols(b)], mean)
        for c in send2(1, b):
            c.start()

    mean = second_heads()
    for b in range(ny):
        second_input(mean, b)
    for i in range(2):
        for j in range(ny):
            reduced2(i, block(j) if i == 0 else j)

    keep_f = pltpu.make_async_copy(SL2.at[0], out_f.at[0, mine], loc_sem.at[7])
    keep_b = pltpu.make_async_copy(SL2.at[1], out_b.at[0, mine], loc_sem.at[8])
    keep_f.start()
    keep_b.start()

    for n in range(2 * PARTS):
        finish_own(n)
        for j in range(ny - 1):
            finish_line(j, n)

    @pl.when(end)
    def _():
        guest_stash.wait_send()
        guest_frames.wait_send()

    for i in range(2):
        pl.when(goes[i])(lambda: hop1(i, 0).wait_send())
        pl.when(also(edge[i], end))(lambda: guest_in[i].wait_send())

        @pl.when(between)
        def _():
            for c in spread1(i):
                c.wait_send()

            for b in range(ny):
                for c in send1(i, b):
                    c.wait_send()
                for g in range(2):
                    pl.when(goes[i])(lambda: hop2(i, g, b).wait_send())

        for b in range(ny):
            for c in send2(i, b):
                c.wait_send()

            @pl.when(comes[i])
            def _():
                for c in spread(2 + i, HOP2.at[i], second_in[i], b):
                    c.wait_send()

    for i, out in ((0, out_f), (1, out_b)):
        for b in range(ny):
            for c in spread_in(4 + i, out.at[0], b):
                c.wait_recv()
            for c in spread(4 + i, SL2.at[i], out.at[0], b):
                c.wait_send()
    keep_f.wait()
    keep_b.wait()


def body(fresh, sent, stash, returned, loss_grads, plan, frame_ids, qkv_weight, out_weight):
    nt_ = lax.axis_size("tensor")
    n_fsdp = lax.axis_size("fsdp")
    ny = n_fsdp // 2
    _, rows, width = sent.shape
    depth, columns = qkv_weight.shape[1:]
    inner = out_weight.shape[2]
    kh = (columns - inner) // (2 * HS)
    group = inner // HS // kh
    cut = rows // nt_
    dma = pltpu.SemaphoreType.DMA
    anywhere = pl.BlockSpec(memory_space=pl.ANY)
    whole = pl.BlockSpec(memory_space=pltpu.VMEM)
    act = pltpu.VMEM((rows, width), BF)
    acts = pltpu.VMEM((2, rows, width), BF)
    return pl.pallas_call(
        kernel,
        out_shape=[jax.ShapeDtypeStruct(sent.shape, BF)] * 2,
        in_specs=[anywhere] * 5 + [pl.BlockSpec(memory_space=pltpu.SMEM), whole] + [anywhere] * 2,
        out_specs=[anywhere] * 2,
        scratch_shapes=[
            pltpu.VMEM((n_fsdp * depth, columns), BF),
            pltpu.VMEM((n_fsdp * depth, inner), BF),
            pltpu.VMEM((columns, n_fsdp * depth), BF),
            acts, acts, acts, act, act, act, acts,
            pltpu.VMEM(frame_ids.shape, jnp.int32),
            pltpu.VMEM((5 * rows, width), BF),
            pltpu.VMEM((3, rows, HS), F32),
            pltpu.VMEM((5 * rows, columns), BF),
            pltpu.VMEM((3, kh, group * rows, rows), F32),
            pltpu.VMEM((2 * rows, inner), BF),
            pltpu.VMEM((2 * rows, columns), BF),
            pltpu.VMEM((2 * rows, inner), F32),
            pltpu.VMEM((2, 2, rows, width), BF),
            pltpu.VMEM((2, nt_ - 1, 2, cut, width), BF),
            pltpu.VMEM((2, 2, cut, width), BF),
            pltpu.VMEM((2, 2, cut, width), BF),
            pltpu.VMEM((2, rows, width), BF),
            pltpu.VMEM((2, nt_ - 1, cut, width), BF),
            pltpu.VMEM((2, cut, width), BF),
            pltpu.VMEM((2, cut, width), BF),
            dma((3, 2 * PARTS)),
            dma((2, ny - 1, 2 * PARTS)),
            dma((2, ny - 1, 2 * PARTS)),
            dma((2, ny - 1, 2 * PARTS)),
            dma((2, ny, 2 * PARTS)),
            dma((9,)),
            dma((4,)),
            dma((2,)),
            dma((2,)),
            dma((2, 2)),
            dma((2, 2, ny)),
            dma((2, ny)),
            dma((6, nt_ - 1, ny)),
            dma((6, nt_ - 1, ny)),
            dma((4, nt_ - 1, ny)),
            dma((4, nt_ - 1, ny)),
            pltpu.SemaphoreType.REGULAR,
        ],
        compiler_params=pltpu.CompilerParams(
            collective_id=0, has_side_effects=True, vmem_limit_bytes=60 << 20
        ),
        name="relay",
    )(fresh, sent, stash, returned, loss_grads, plan, frame_ids, qkv_weight, out_weight)


def solution(mesh):
    placed = (
        P(None, "fsdp", None),
        P("section", "fsdp", None),
        P("section", None, "fsdp", None),
        P("section", "fsdp", None),
        P(None, "fsdp", None),
        P("section", None),
        P(None, "fsdp"),
        P("section", "fsdp", "tensor"),
        P("section", "fsdp", "tensor"),
    )
    return jax.shard_map(
        body,
        mesh=mesh,
        in_specs=placed,
        out_specs=(P("section", "fsdp", None), P("section", "fsdp", None)),
        check_vma=False,
    )
```
